32 devices in a mesh: dp: 8 (over y, x, core), group: 4 (over z).
Axes of the slice: x: 2, y: 2, z: 4, core: 2. Of those that a mesh axis runs over, the one named last changes fastest.
Arguments:
- act_query: bfloat16 [8192, 768], P(('dp', 'group')), may hold values from -6 to 6
- grad_query: bfloat16 [8192, 768], P(('dp', 'group')), may hold values from -6 to 6
- act_keyval: bfloat16 [8192, 768], P(('dp', 'group')), may hold values from -6 to 6
- grad_keyval: bfloat16 [8192, 128], P(('dp', 'group')), may hold values from -6 to 6
- sample_rows: int32 [4096], P(('dp', 'group')), may hold values from 0 to 255
- state_aq: float32 [768, 768], P('dp'), as said below
- state_gq: float32 [768, 768], P('dp'), as said below
- state_akv: float32 [768, 768], P('dp'), as said below
- state_gkv: float32 [128, 128], P('dp'), as said below
- weight_query: float32 [768, 768], P('dp'), may hold values from -0.21875 to 0.21875
- weight_keyval: float32 [768, 128], P('dp'), may hold values from -0.21875 to 0.21875
- moment_query: float32 [768, 768], P('dp'), may hold values from -6 to 6
- moment_keyval: float32 [768, 128], P('dp'), may hold values from -6 to 6
Outputs:
- new_state_aq: float32 [768, 768], P('dp')
- new_state_gq: float32 [768, 768], P('dp')
- new_state_akv: float32 [768, 768], P('dp')
- new_state_gkv: float32 [128, 128], P('dp')
- new_weight_query: float32 [768, 768], P('dp')
- new_weight_keyval: float32 [768, 128], P('dp')
- new_moment_query: float32 [768, 768], P('dp')
- new_moment_keyval: float32 [768, 128], P('dp')
The draws below stay inside these ranges and needn't reach their ends.
Inputs may be any that keep to these rules, and one draw needn't show every extreme that they name: `sample_rows`: each entry indexes one of the 256 tokens of the device that holds it. `state_aq`: symmetric positive definite. `state_gq`: symmetric positive definite. `state_akv`: symmetric positive definite. `state_gkv`: symmetric positive definite.
All inputs are finite; a program needn't handle non-finite values. Where the reference program divides by a largest or mean magnitude, that divisor is 1e-20 or more.
Results may differ from the reference program's by a relative error of at most 0.0003.
Values sent between devices are 32-bit elements; how exact they have to be, the bound alone decides.
No kernel may reach another device: no remote copies, remote signals or barrier semaphores. Data moves between devices by JAX's collectives and lax.ppermute only.
A program may use at most 128 MiB of HBM per device.

```python
import jax
import jax.numpy as jnp
from jax import lax

D = 768
KV = 128
TOK_DEV = 256
NS_ITERS = 2
SAMP = 128
ROWS = 8192
SAMPLES = 4096
N_DP = 8
N_GROUP = 4


def spd_factor(key, extent):
    key_off, key_diag = jax.random.split(key)
    uniform_part = jax.random.uniform(key_off, (extent, extent), jnp.float32, -1.0, 1.0)
    symmetric = (uniform_part + uniform_part.T) * (0.5 / extent)
    identity = jnp.eye(extent, dtype=jnp.float32)
    diagonal_part = jax.random.uniform(key_diag, (extent,), jnp.float32, 1.0, 2.0)
    return symmetric * (1.0 - identity) + identity * diagonal_part[None, :]


def draw_state_aq(key, part):
    return spd_factor(jax.random.fold_in(key, 11), D)


def draw_state_gq(key, part):
    return spd_factor(jax.random.fold_in(key, 12), D)


def draw_state_akv(key, part):
    return spd_factor(jax.random.fold_in(key, 13), D)


def draw_state_gkv(key, part):
    return spd_factor(jax.random.fold_in(key, 14), KV)


def touch_ends(entries, stream_key, smallest, largest):
    place = [jax.random.randint(jax.random.fold_in(stream_key, axis), (), 0, length) for axis, length in enumerate(entries.shape)]
    widest = entries.shape.index(max(entries.shape))
    beside = place[:widest] + [(place[widest] + 1) % entries.shape[widest]] + place[widest + 1:]
    return entries.at[tuple(place)].set(smallest).at[tuple(beside)].set(largest)


def with_spikes(drawn, stream_key, source, target, parts, factor):
    def block_of(axis_at):
        return (jnp.arange(drawn.shape[axis_at]) // (drawn.shape[axis_at] // parts)).reshape((-1,) + (1,) * (drawn.ndim - 1 - axis_at))

    near = jax.random.permutation(stream_key, parts)[block_of(target)]
    other_side = (block_of(target) + parts // 2) % parts
    return jnp.where((block_of(source) == near) | (block_of(source) == other_side), factor * drawn, drawn)


def block_scale(key, shape, cuts, low, top_value):
    gain, own = 1.0, jax.random.fold_in(key, 6)
    for position, blocks in cuts:
        heights = jnp.exp(jax.random.uniform(jax.random.fold_in(own, position), (blocks,), jnp.float32, low / len(cuts), top_value / len(cuts)))
        gain = gain * jnp.repeat(heights, shape[position] // blocks).reshape([-1 if axis == position else 1 for axis in range(len(shape))])
    return gain


def bell_draw(stream_key, shape, width, most, cuts=(), held_as=jnp.bfloat16):
    level = block_scale(stream_key, shape, cuts, -0.22, 0.18) if cuts else 1.0
    values = jax.random.normal(stream_key, shape, jnp.float32) * width * level
    return jnp.minimum(jnp.maximum(values, -most), most).astype(held_as)


def heavy_noise(rng, shape, deviation, reach, shards, heavy, kind=jnp.bfloat16):
    drawn = deviation * jax.random.normal(rng, shape, jnp.float32)
    if shards:
        drawn = drawn * block_scale(rng, shape, shards, -0.22, 0.18)
    return jnp.clip(with_spikes(drawn, jax.random.fold_in(rng, 3), *heavy), -reach, reach).astype(kind)


def setup_inputs(seed: int = 0) -> dict:
    splits = jax.random.split(jax.random.key(seed), 14)
    return {
        "act_query": heavy_noise(splits[0], (ROWS, D), 1.0, 6.0, ((0, 32),), (0, 1, 32, 2.75)),
        "grad_query": heavy_noise(splits[1], (ROWS, D), 1.0, 6.0, ((0, 32),), (0, 1, 32, 2.75)),
        "act_keyval": heavy_noise(splits[2], (ROWS, D), 1.0, 6.0, ((0, 32),), (0, 1, 32, 2.75)),
        "grad_keyval": heavy_noise(splits[3], (ROWS, KV), 1.0, 6.0, ((0, 32),), (0, 1, 32, 2.75)),
        "sample_rows": touch_ends(jax.random.randint(splits[4], (SAMPLES,), 0, TOK_DEV), jax.random.fold_in(splits[4], 1), 0, TOK_DEV - 1).astype(jnp.int32),
        "state_aq": draw_state_aq(jax.random.fold_in(splits[13], 71), 0),
        "state_gq": draw_state_gq(jax.random.fold_in(splits[13], 71), 0),
        "state_akv": draw_state_akv(jax.random.fold_in(splits[13], 71), 0),
        "state_gkv": draw_state_gkv(jax.random.fold_in(splits[13], 71), 0),
        "weight_query": bell_draw(splits[9], (D, D), D ** -0.5, 0.21875, ((0, 8),), jnp.float32),
        "weight_keyval": bell_draw(splits[10], (D, KV), D ** -0.5, 0.21875, ((0, 8),), jnp.float32),
        "moment_query": bell_draw(splits[11], (D, D), 1.0, 6.0, ((0, 8),), jnp.float32),
        "moment_keyval": bell_draw(splits[12], (D, KV), 1.0, 6.0, ((0, 8),), jnp.float32),
    }


PRECISE = lax.Precision.HIGHEST
BLEND_RATE = 0.8
DAMPING = 0.05
MOMENTUM = 0.9
LEARNING_RATE = 0.001
TRUST_BOUND = 0.5

def newton(damped):
    extent = damped.shape[0]
    identity = jnp.eye(extent, dtype=jnp.float32)
    inverse_norm = 1.0 / jnp.max(lax.optimization_barrier(jnp.sum(jnp.abs(damped), axis=1)))
    iterate = inverse_norm * (2.0 * identity - inverse_norm * damped)
    for sweep in range(NS_ITERS - 1):
        product = jnp.dot(damped, iterate, precision=PRECISE)
        iterate = jnp.dot(iterate, 2.0 * identity - product, precision=PRECISE)
    return iterate

def damped_inverse(factor):
    extent = factor.shape[0]
    identity = jnp.eye(extent, dtype=jnp.float32)
    return newton(factor + DAMPING * jnp.trace(factor) / extent * identity)

def precondition(left_inverse, gradient, right_inverse):
    return jnp.dot(jnp.dot(left_inverse, gradient, precision=PRECISE), right_inverse, precision=PRECISE)

def inner_rows(first_block, second_block):
    return lax.dot_general(first_block, second_block, (((0,), (0,)), ((), ())), preferred_element_type=jnp.float32)

def reference(act_query, grad_query, act_keyval, grad_keyval, sample_rows, state_aq, state_gq, state_akv, state_gkv, weight_query, weight_keyval, moment_query, moment_keyval):
    devices = N_DP * N_GROUP
    total_samples = SAMP * devices
    picked = jnp.arange(total_samples, dtype=jnp.int32) // SAMP * TOK_DEV + sample_rows.astype(jnp.int32)

    def covariance(tokens_block):
        chosen = tokens_block[picked]
        return inner_rows(chosen, chosen) / total_samples
    sum_q = inner_rows(act_query, grad_query)
    sum_kv = inner_rows(act_keyval, grad_keyval)
    new_aq = BLEND_RATE * state_aq + (1.0 - BLEND_RATE) * covariance(act_query)
    new_gq = BLEND_RATE * state_gq + (1.0 - BLEND_RATE) * covariance(grad_query)
    new_akv = BLEND_RATE * state_akv + (1.0 - BLEND_RATE) * covariance(act_keyval)
    new_gkv = BLEND_RATE * state_gkv + (1.0 - BLEND_RATE) * covariance(grad_keyval)
    step_q = precondition(damped_inverse(new_aq), sum_q, damped_inverse(new_gq))
    step_kv = precondition(damped_inverse(new_akv), sum_kv, damped_inverse(new_gkv))
    fitness = jnp.sum(step_q * sum_q) + jnp.sum(step_kv * sum_kv)
    scale = jnp.sqrt(TRUST_BOUND / (LEARNING_RATE * LEARNING_RATE * fitness))
    moment_q = MOMENTUM * moment_query + scale * step_q
    moment_kv = MOMENTUM * moment_keyval + scale * step_kv
    weight_q = weight_query - LEARNING_RATE * moment_q
    weight_kv = weight_keyval - LEARNING_RATE * moment_kv
    return (new_aq, new_gq, new_akv, new_gkv, weight_q, weight_kv, moment_q, moment_kv)
```

```python
import functools

import jax
import jax.numpy as jnp
from jax import lax
from jax.experimental import pallas as pl
from jax.experimental.pallas import tpu as pltpu
from jax.sharding import PartitionSpec as P

PRECISE = lax.Precision.HIGHEST
BLEND_RATE = 0.8
DAMPING = 0.05
MOMENTUM = 0.9
LEARNING_RATE = 0.001
TRUST_BOUND = 0.5
LANES = 128
F32 = jnp.float32
BF16 = jnp.bfloat16
VMEM_LIMIT = 48 * 1024 * 1024


def rolled(block, shift):
    return pltpu.roll(block, shift, 1)


def window_tiles(block, start, width):
    extent = block.shape[1]
    shift = lax.rem(extent - start, extent)
    turned = rolled(block, shift)
    return [turned[:, LANES * t:LANES * (t + 1)] for t in range(width // LANES)]


def plain_tiles(block):
    return [block[:, LANES * t:LANES * (t + 1)] for t in range(block.shape[1] // LANES)]


def write_tiles(ref, lead, tiles, at=0):
    for tile in tiles:
        ref[lead, at:at + tile.shape[0], :] = tile
        at += tile.shape[0]
    return at


def product(first, second):
    return lax.dot_general(
        first, second, (((1,), (0,)), ((), ())), preferred_element_type=F32
    )


def gram_kernel(
    n, k, width, scale,
    pos, rows_own, rows_other, aq, gq, akv, gkv, other, st_aq, st_gq, st_akv, st_gkv,
    a_send, a_keep, b_send, b_keep, s_send, s_keep, k_send, k_keep,
    t_q, t_kv, u_aq, u_gq, u_akv, u_gkv, g_kv,
):
    q, c = pos[0], pos[1]
    D = aq.shape[1]
    tokens = aq.shape[0]
    samples = rows_own.shape[1]

    def picker(rows):
        token = lax.broadcasted_iota(jnp.int32, (tokens, samples), 0)
        return (token == rows[...]).astype(F32).T.astype(BF16)

    pick_own, pick_other = picker(rows_own), picker(rows_other)

    def both(own, lo, hi):
        return jnp.concatenate([own[...], other[:, lo:hi].astype(BF16)], axis=0)

    def sampled(own, lo, hi):
        return jnp.concatenate(
            [product(pick_own, own[...]), product(pick_other, other[:, lo:hi].astype(BF16))],
            axis=0,
        )

    def turn(ref, values):
        ref[...] = values.astype(F32).T.astype(BF16)

    y_aq = sampled(aq, 0, D)
    y_gq = sampled(gq, D, 2 * D)
    y_akv = sampled(akv, 2 * D, 3 * D)
    y_gkv = sampled(gkv, 3 * D, 3 * D + gkv.shape[1])
    turn(u_aq, y_aq)
    turn(u_gq, y_gq)
    turn(u_akv, y_akv)
    turn(u_gkv, y_gkv)
    turn(t_q, both(aq, 0, D))
    turn(t_kv, both(akv, 2 * D, 3 * D))
    y_aq, y_gq = y_aq.astype(BF16), y_gq.astype(BF16)
    y_akv, y_gkv = y_akv.astype(BF16), y_gkv.astype(BF16)

    blocks = [2 * jnp.bitwise_xor(q, r) + c for r in range(4)]

    def left(ref):
        parts = [ref[pl.ds(pl.multiple_of(n * b, 32), n), :] for b in blocks]
        return jnp.concatenate(parts, axis=0)

    def four(values):
        return [values[n * r:n * (r + 1)] for r in range(4)]

    share = BLEND_RATE / 4.0

    def window(values, r):
        return window_tiles(values, n * blocks[r], width)

    def place(send, keep, first, tiles, at=0):
        second = 3 - first
        write_tiles(send, 0, tiles[first], at)
        write_tiles(send, 1, tiles[3], at)
        write_tiles(keep, 0, tiles[0], at)
        return write_tiles(keep, 1, tiles[second], at)

    def factor(ref, y, state):
        parts = four(product(left(ref), y) * scale)
        parts[0] = parts[0] + share * state[...]
        return [window(parts[r], r) for r in range(4)]

    place(a_send, a_keep, 1, factor(u_aq, y_aq, st_aq))
    place(b_send, b_keep, 2, factor(u_gq, y_gq, st_gq))
    sum_q = four(product(left(t_q), both(gq, D, 2 * D)))
    place(s_send, s_keep, 1, [plain_tiles(part) for part in sum_q])
    at = place(k_send, k_keep, 2, factor(u_akv, y_akv, st_akv))
    sum_kv = four(product(left(t_kv), both(gkv, 3 * D, 3 * D + gkv.shape[1])))
    at = place(k_send, k_keep, 2, [plain_tiles(part) for part in sum_kv], at)
    g_kv[...] = product(u_gkv[...], y_gkv) * scale
    small = [g_kv[pl.ds(pl.multiple_of(k * b, 8), k), :] for b in blocks]
    small[0] = small[0] + share * st_gkv[...]
    place(k_send, k_keep, 2, [[part] for part in small], at)


def identity_rows(rows, extent, start):
    row = lax.broadcasted_iota(jnp.int32, (rows, extent), 0) + start
    column = lax.broadcasted_iota(jnp.int32, (rows, extent), 1)
    return row == column


def scaled_inverse_terms(matrix):
    extent = matrix.shape[0]
    on_diagonal = identity_rows(extent, extent, 0)
    trace = jnp.sum(jnp.where(on_diagonal, matrix, 0.0))
    damped = matrix + jnp.where(on_diagonal, DAMPING * trace / extent, 0.0)
    c = 1.0 / jnp.max(jnp.sum(jnp.abs(damped), axis=1))
    return c, c * damped


def halves(values):
    high = values.astype(BF16)
    return high, (values - high.astype(F32)).astype(BF16)


def times(values, high, low):
    v_high, v_low = halves(values)
    rows = values.shape[0]
    stacked = product(jnp.concatenate([v_high, v_low], axis=0), high)
    return stacked[:rows] + stacked[rows:] + product(v_high, low)


def piece_blocks(q, c):
    own = [2 * jnp.bitwise_xor(q, r) + c for r in range(4)]
    other = [2 * jnp.bitwise_xor(q, r) + (1 - c) for r in range(4)]
    return own + other


def assemble(pieces, blocks, n, width, extent, whole):
    tiles = width // LANES
    for piece, b in zip(pieces, blocks):
        parts = [piece[n * t:n * (t + 1), :] for t in range(tiles)]
        parts += [jnp.zeros((n, LANES), F32)] * (extent // LANES - tiles)
        turned = rolled(jnp.concatenate(parts, axis=1), n * b)
        whole[pl.ds(pl.multiple_of(n * b, 8), n), :] = turned
    windows = whole[...]

    def block_of(axis):
        shape = (extent, 1) if axis == 0 else (1, extent)
        index = lax.broadcasted_iota(jnp.int32, shape, axis)
        return sum([(index >= n * step).astype(jnp.int32) for step in range(1, 8)])

    apart = jnp.bitwise_and(block_of(1) - block_of(0), 7)
    matrix = jnp.where(apart <= 4, windows, windows.T)
    return matrix


def own_rows(ref, q, c, n):
    return ref[pl.ds(pl.multiple_of(n * (2 * q + c), 8), n), :]


def left_rows(c, rows, start, high, low):
    first = jnp.where(identity_rows(rows.shape[0], rows.shape[1], start), 2.0, 0.0) - rows
    second = times(first, high, low)
    third = 2.0 * second - times(second, high, low)
    return c * (2.0 * first - third)


def right_product(values, c, high, low):
    first = 2.0 * values - times(values, high, low)
    second = times(first, high, low)
    third = 2.0 * second - times(second, high, low)
    return c * (2.0 * first - third)


def left_kernel(n, width, pos, *refs):
    pieces, (new_ref, x_ref, whole, high_ref, low_ref) = refs[:8], refs[8:]
    q, c = pos[0], pos[1]
    extent = whole.shape[0]
    matrix = assemble(pieces, piece_blocks(q, c), n, width, extent, whole)
    whole[...] = matrix
    new_ref[...] = own_rows(whole, q, c, n)
    factor, scaled = scaled_inverse_terms(matrix)
    whole[...] = scaled
    high_ref[...], low_ref[...] = halves(scaled)
    x_ref[...] = left_rows(
        factor, own_rows(whole, q, c, n), n * (2 * q + c), high_ref[...], low_ref[...]
    )


def middle_kernel(n, pos, x_ref, *refs):
    pieces, (t_ref, high_ref, low_ref) = refs[:8], refs[8:]
    q, c = pos[0], pos[1]
    tiles = high_ref.shape[1] // LANES
    for piece, b in zip(pieces, piece_blocks(q, c)):
        rows = jnp.concatenate([piece[n * t:n * (t + 1), :] for t in range(tiles)], axis=1)
        at = pl.ds(pl.multiple_of(n * b, 32), n)
        high_ref[at, :], low_ref[at, :] = halves(rows)
    t_ref[...] = times(x_ref[...], high_ref[...], low_ref[...])


def right_kernel(n, width, pos, t_ref, s_own, *refs):
    pieces, (new_ref, step_ref, fit_ref, whole, high_ref, low_ref) = refs[:8], refs[8:]
    q, c = pos[0], pos[1]
    extent = whole.shape[0]
    matrix = assemble(pieces, piece_blocks(q, c), n, width, extent, whole)
    whole[...] = matrix
    new_ref[...] = own_rows(whole, q, c, n)
    factor, scaled = scaled_inverse_terms(matrix)
    high_ref[...], low_ref[...] = halves(scaled)
    step = right_product(t_ref[...], factor, high_ref[...], low_ref[...])
    step_ref[...] = step
    tiles = extent // LANES
    gradient = jnp.concatenate([s_own[n * t:n * (t + 1), :] for t in range(tiles)], axis=1)
    fit_ref[...] = jnp.broadcast_to(jnp.sum(step * gradient), fit_ref.shape)


def keyval_kernel(n, k, width, pos, *refs):
    pieces = refs[:8]
    new_left, new_right, step_ref, fit_ref = refs[8:12]
    whole, high_ref, low_ref, grad_ref, g_ref = refs[12:]
    q, c = pos[0], pos[1]
    extent = whole.shape[0]
    blocks = piece_blocks(q, c)
    base = n * (width // LANES)
    for piece, b in zip(pieces, blocks):
        grad_ref[pl.ds(pl.multiple_of(n * b, 8), n), :] = piece[base:base + n, :]
        g_ref[pl.ds(pl.multiple_of(k * b, 8), k), :] = piece[base + n:base + n + k, :]
    matrix = assemble(pieces, blocks, n, width, extent, whole)
    whole[...] = matrix
    new_left[...] = own_rows(whole, q, c, n)
    new_right[...] = own_rows(g_ref, q, c, k)
    factor, scaled = scaled_inverse_terms(matrix)
    whole[...] = scaled
    high_ref[...], low_ref[...] = halves(scaled)
    x_rows = left_rows(
        factor, own_rows(whole, q, c, n), n * (2 * q + c), high_ref[...], low_ref[...]
    )
    t_rows = times(x_rows, *halves(grad_ref[...]))
    factor, scaled = scaled_inverse_terms(g_ref[...])
    step = right_product(t_rows, factor, *halves(scaled))
    step_ref[...] = step
    fit_ref[...] = jnp.broadcast_to(jnp.sum(step * own_rows(grad_ref, q, c, n)), fit_ref.shape)


def call(kernel, outs, scratch, count, flops=0):
    vmem = pl.BlockSpec(memory_space=pltpu.VMEM)
    smem = pl.BlockSpec(memory_space=pltpu.SMEM)
    return pl.pallas_call(
        kernel,
        out_shape=[jax.ShapeDtypeStruct(shape, F32) for shape in outs],
        in_specs=[smem] + [vmem] * (count - 1),
        out_specs=[vmem] * len(outs),
        scratch_shapes=[pltpu.VMEM(shape, kind) for shape, kind in scratch],
        compiler_params=pltpu.CompilerParams(vmem_limit_bytes=VMEM_LIMIT),
        cost_estimate=pl.CostEstimate(flops=flops, bytes_accessed=4_000_000, transcendentals=0),
    )


def flip(value, bit, axis="dp", size=8):
    return lax.ppermute(value, axis, [(i, i ^ bit) for i in range(size)])


def reduce_piece(send, keep, first, second):
    came = flip(send, first)
    partial = keep[1] + came[1]
    return (keep[0] + came[0]) + flip(partial, second)


def reduce_planes(piece, first, second):
    piece = piece + flip(piece, first, "group", 4)
    return piece + flip(piece, second, "group", 4)


def spread(piece, x_bit, first, second):
    near = flip(piece, first)
    across = flip(piece, second)
    far = flip(across, first)
    own = {0: piece, first: near, second: across, first | second: far}
    ordered = [own[r << 1] for r in range(4)]
    return ordered + [flip(value, 1) for value in ordered]


def fast_shards(
    act_query, grad_query, act_keyval, grad_keyval, sample_rows,
    state_aq, state_gq, state_akv, state_gkv,
    weight_query, weight_keyval, moment_query, moment_keyval,
):
    D, KV = act_query.shape[1], grad_keyval.shape[1]
    n, k = state_aq.shape[0], state_gkv.shape[0]
    tokens, samples = act_query.shape[0], sample_rows.shape[0]
    width = -(-5 * n // LANES) * LANES
    d = lax.axis_index("dp")
    pos = jnp.stack([d // 2, d % 2]).astype(jnp.int32)
    scale = (1.0 - BLEND_RATE) / (samples * 32)

    mine = jnp.concatenate([act_query, grad_query, act_keyval, grad_keyval], axis=1).astype(F32)
    other = flip(mine, 1)
    rows_own = sample_rows.reshape(1, samples)
    rows_other = flip(rows_own, 1)

    r_f, r_s = n * (width // LANES), n * (D // LANES)
    r_k = r_f + n * (KV // LANES) + k
    outs = []
    for rows in (r_f, r_f, r_s, r_k):
        outs += [(2, rows, LANES)] * 2
    grams = call(
        functools.partial(gram_kernel, n, k, width, scale),
        outs,
        [
            ((D, 2 * tokens), BF16), ((D, 2 * tokens), BF16),
            ((D, 2 * samples), BF16), ((D, 2 * samples), BF16), ((D, 2 * samples), BF16),
            ((KV, 2 * samples), BF16), ((KV, KV), F32),
        ],
        12,
        2_000_000_000,
    )(
        pos, rows_own, rows_other, act_query, grad_query, act_keyval, grad_keyval, other,
        state_aq, state_gq, state_akv, state_gkv,
    )
    X, Y = 2, 4
    own_a = reduce_piece(grams[0], grams[1], X, Y)
    own_b = reduce_piece(grams[2], grams[3], Y, X)
    own_s = reduce_piece(grams[4], grams[5], X, Y)
    own_k = reduce_piece(grams[6], grams[7], Y, X)
    own_a = reduce_planes(own_a, 1, 2)
    own_b = reduce_planes(own_b, 2, 1)
    own_s = reduce_planes(own_s, 1, 2)
    own_k = reduce_planes(own_k, 2, 1)
    all_a = spread(own_a, X, X, Y)
    all_b = spread(own_b, X, Y, X)
    all_s = spread(own_s, X, X, Y)
    all_k = spread(own_k, X, Y, X)

    square = [((D, D), F32), ((D, D), BF16), ((D, D), BF16)]
    fit = (8, LANES)
    new_aq, x_rows = call(
        functools.partial(left_kernel, n, width), [(n, D)] * 2, square, 9, 700_000_000
    )(pos, *all_a)
    (t_rows,) = call(
        functools.partial(middle_kernel, n), [(n, D)], square[1:], 10, 350_000_000
    )(pos, x_rows, *all_s)
    new_gq, step_q, fit_q = call(
        functools.partial(right_kernel, n, width), [(n, D), (n, D), fit], square, 11, 1_000_000_000
    )(pos, t_rows, own_s, *all_b)
    new_akv, new_gkv, step_kv, fit_kv = call(
        functools.partial(keyval_kernel, n, k, width),
        [(n, D), (k, KV), (n, KV), fit],
        square + [((D, KV), F32), ((KV, KV), F32)],
        9,
        1_000_000_000,
    )(pos, *all_k)

    total = fit_q + fit_kv
    for bit in (1, 2, 4):
        total = total + flip(total, bit)
    fitness = total[0, 0]
    scale = jnp.sqrt(TRUST_BOUND / (LEARNING_RATE * LEARNING_RATE * fitness))
    moment_q = MOMENTUM * moment_query + scale * step_q
    moment_kv = MOMENTUM * moment_keyval + scale * step_kv
    weight_q = weight_query - LEARNING_RATE * moment_q
    weight_kv = weight_keyval - LEARNING_RATE * moment_kv
    return (new_aq, new_gq, new_akv, new_gkv, weight_q, weight_kv, moment_q, moment_kv)


def from_root(value, axis, source):
    kept = jnp.where(lax.axis_index(axis) == source, value, 0).astype(value.dtype)
    return lax.psum(kept, axis)


def newton(damped):
    extent = damped.shape[0]
    identity = jnp.eye(extent, dtype=jnp.float32)
    inverse_norm = 1.0 / jnp.max(jnp.sum(jnp.abs(damped), axis=1))
    iterate = inverse_norm * (2.0 * identity - inverse_norm * damped)
    product = jnp.dot(damped, iterate, precision=PRECISE)
    iterate = jnp.dot(iterate, 2.0 * identity - product, precision=PRECISE)
    return iterate


def damped_inverse(factor):
    extent = factor.shape[0]
    identity = jnp.eye(extent, dtype=jnp.float32)
    return newton(factor + DAMPING * jnp.trace(factor) / extent * identity)


def precondition(left_inverse, gradient, right_inverse):
    return jnp.dot(
        jnp.dot(left_inverse, gradient, precision=PRECISE), right_inverse, precision=PRECISE
    )


def inner_rows(first_block, second_block):
    return lax.dot_general(
        first_block, second_block, (((0,), (0,)), ((), ())), preferred_element_type=jnp.float32
    )


def deliver(matrix, holder):
    return from_root(matrix, ("dp", "group"), holder)


def owner_step(left_factor, right_factor, gradient):
    return precondition(damped_inverse(left_factor), gradient, damped_inverse(right_factor))


def shards(
    act_query,
    grad_query,
    act_keyval,
    grad_keyval,
    sample_rows,
    state_aq,
    state_gq,
    state_akv,
    state_gkv,
    weight_query,
    weight_keyval,
    moment_query,
    moment_keyval,
):
    devices = lax.axis_size("dp") * lax.axis_size("group")
    total_samples = sample_rows.shape[0] * devices
    flat_index = lax.axis_index("dp") * lax.axis_size("group") + lax.axis_index("group")
    extent = state_aq.shape[0]
    start = lax.axis_index("dp") * extent

    def covariance(tokens_block):
        chosen = jnp.take(tokens_block, sample_rows, axis=0)
        return inner_rows(chosen, chosen)

    local_terms = (
        covariance(act_query),
        covariance(grad_query),
        covariance(act_keyval),
        covariance(grad_keyval),
        inner_rows(act_query, grad_query),
        inner_rows(act_keyval, grad_keyval),
    )
    shares = (
        lax.psum_scatter(local_terms[0], "dp", scatter_dimension=0, tiled=True),
        lax.psum_scatter(local_terms[1], "dp", scatter_dimension=0, tiled=True),
        lax.psum_scatter(local_terms[2], "dp", scatter_dimension=0, tiled=True),
        lax.psum_scatter(local_terms[3], "dp", scatter_dimension=0, tiled=True),
        lax.psum_scatter(local_terms[4], "dp", scatter_dimension=0, tiled=True),
        lax.psum_scatter(local_terms[5], "dp", scatter_dimension=0, tiled=True),
    )
    totals = lax.psum((shares[0], shares[1], shares[2], shares[3], shares[4], shares[5]), "group")
    cov_aq, cov_gq, cov_akv, cov_gkv, rows_q, rows_kv = totals
    new_aq = BLEND_RATE * state_aq + (1.0 - BLEND_RATE) * (cov_aq / total_samples)
    new_gq = BLEND_RATE * state_gq + (1.0 - BLEND_RATE) * (cov_gq / total_samples)
    new_akv = BLEND_RATE * state_akv + (1.0 - BLEND_RATE) * (cov_akv / total_samples)
    new_gkv = BLEND_RATE * state_gkv + (1.0 - BLEND_RATE) * (cov_gkv / total_samples)
    gathered = (
        lax.all_gather(new_aq, "dp", axis=0, tiled=True),
        lax.all_gather(new_gq, "dp", axis=0, tiled=True),
        lax.all_gather(new_akv, "dp", axis=0, tiled=True),
        lax.all_gather(new_gkv, "dp", axis=0, tiled=True),
        lax.all_gather(rows_q, "dp", axis=0, tiled=True),
        lax.all_gather(rows_kv, "dp", axis=0, tiled=True),
    )
    whole_aq, whole_gq, whole_akv, whole_gkv, whole_sum_q, whole_sum_kv = gathered
    holders = (0, 0, 1, 1)
    pairs = (
        (whole_aq, whole_gq, whole_sum_q, rows_q, holders[0], holders[1]),
        (whole_akv, whole_gkv, whole_sum_kv, rows_kv, holders[2], holders[3]),
    )
    step_rows = []
    fitness = jnp.zeros((), jnp.float32)
    for left_factor, right_factor, gradient, gradient_rows, left_holder, right_holder in pairs:
        whole_step = lax.cond(
            flat_index == left_holder,
            owner_step,
            lambda first, second, third: jnp.zeros_like(third),
            left_factor,
            right_factor,
            gradient,
        )
        whole_step = deliver(whole_step, left_holder)
        fitness = fitness + jnp.sum(whole_step * gradient)
        step_rows.append(lax.dynamic_slice_in_dim(whole_step, start, extent, 0))
    scale = jnp.sqrt(TRUST_BOUND / (LEARNING_RATE * LEARNING_RATE * fitness))
    moment_q = MOMENTUM * moment_query + scale * step_rows[0]
    moment_kv = MOMENTUM * moment_keyval + scale * step_rows[1]
    weight_q = weight_query - LEARNING_RATE * moment_q
    weight_kv = weight_keyval - LEARNING_RATE * moment_kv
    return (new_aq, new_gq, new_akv, new_gkv, weight_q, weight_kv, moment_q, moment_kv)


def solution(mesh):
    placed = (
        P(("dp", "group"), None),
        P(("dp", "group"), None),
        P(("dp", "group"), None),
        P(("dp", "group"), None),
        P(("dp", "group")),
        P("dp", None),
        P("dp", None),
        P("dp", None),
        P("dp", None),
        P("dp", None),
        P("dp", None),
        P("dp", None),
        P("dp", None),
    )
    plane = mesh.shape["dp"] == 8 and mesh.shape["group"] == 4
    return jax.shard_map(
        fast_shards if plane else shards,
        mesh=mesh,
        in_specs=placed,
        out_specs=(
            P("dp", None),
            P("dp", None),
            P("dp", None),
            P("dp", None),
            P("dp", None),
            P("dp", None),
            P("dp", None),
            P("dp", None),
        ),
        check_vma=False,
    )
```

```python
import functools

import jax
import jax.numpy as jnp
from jax import lax
from jax.experimental import pallas as pl
from jax.experimental.pallas import tpu as pltpu
from jax.sharding import PartitionSpec as P

PRECISE = lax.Precision.HIGHEST
BLEND_RATE = 0.8
DAMPING = 0.05
MOMENTUM = 0.9
LEARNING_RATE = 0.001
TRUST_BOUND = 0.5
LANES = 128
F32 = jnp.float32
BF16 = jnp.bfloat16
VMEM_LIMIT = 48 * 1024 * 1024


def rolled(block, shift):
    return pltpu.roll(block, shift, 1)


def window_tiles(block, start, width):
    extent = block.shape[1]
    shift = lax.rem(extent - start, extent)
    turned = rolled(block, shift)
    return [turned[:, LANES * t:LANES * (t + 1)] for t in range(width // LANES)]


def plain_tiles(block):
    return [block[:, LANES * t:LANES * (t + 1)] for t in range(block.shape[1] // LANES)]


def write_tiles(ref, lead, tiles, at=0):
    for tile in tiles:
        ref[lead, at:at + tile.shape[0], :] = tile
        at += tile.shape[0]
    return at


def product(first, second):
    return lax.dot_general(
        first, second, (((1,), (0,)), ((), ())), preferred_element_type=F32
    )


def cast_kernel(aq, gq, akv, gkv, out):
    at = 0
    for ref in (aq, gq, akv, gkv):
        out[:, at:at + ref.shape[1]] = ref[...].astype(F32)
        at += ref.shape[1]


def picker(rows, tokens):
    token = lax.broadcasted_iota(jnp.int32, (tokens, rows.shape[1]), 0)
    return (token == rows[...]).astype(F32).T.astype(BF16)


def turned(values):
    return values.astype(F32).T.astype(BF16)


def own_kernel(rows, aq, gq, akv, gkv, y_aq, y_gq, y_akv, y_gkv, u_aq, u_gq, u_akv, u_gkv, t_q, t_kv):
    pick = picker(rows, aq.shape[0])
    for source, y, u in ((aq, y_aq, u_aq), (gq, y_gq, u_gq), (akv, y_akv, u_akv), (gkv, y_gkv, u_gkv)):
        chosen = product(pick, source[...])
        y[...] = chosen.astype(BF16)
        u[...] = chosen.T.astype(BF16)
    t_q[...] = turned(aq[...])
    t_kv[...] = turned(akv[...])


def gram_kernel(
    n, k, width, scale,
    pos, rows_other, other, gq, gkv,
    oy_aq, oy_gq, oy_akv, oy_gkv, ou_aq, ou_gq, ou_akv, ou_gkv, ot_q, ot_kv,
    st_aq, st_gq, st_akv, st_gkv,
    a_send, a_keep, b_send, b_keep, c_send, c_keep, d_send, d_keep,
    u_aq, u_gq, u_akv, u_gkv, t_q, t_kv, g_kv,
):
    q, c = pos[0], pos[1]
    tokens, D = gq.shape
    KV = gkv.shape[1]
    samples = oy_aq.shape[0]
    pick = picker(rows_other, tokens)

    def theirs(lo, hi):
        return other[:, lo:hi].astype(BF16)

    def join(u, own_u, own_y, lo, hi):
        chosen = product(pick, theirs(lo, hi))
        u[:, :samples] = own_u[...]
        u[:, samples:] = chosen.T.astype(BF16)
        return jnp.concatenate([own_y[...], chosen.astype(BF16)], axis=0)

    blocks = [2 * jnp.bitwise_xor(q, r) + c for r in range(4)]

    def left(ref):
        parts = [ref[pl.ds(pl.multiple_of(n * b, 32), n), :] for b in blocks]
        return jnp.concatenate(parts, axis=0)

    def four(values):
        return [values[n * r:n * (r + 1)] for r in range(4)]

    share = BLEND_RATE / 4.0

    def place(send, keep, first, tiles, at=0):
        write_tiles(send, 0, tiles[first], at)
        write_tiles(send, 1, tiles[3], at)
        write_tiles(keep, 0, tiles[0], at)
        return write_tiles(keep, 1, tiles[3 - first], at)

    def factor(ref, y, state):
        parts = four(product(left(ref), y) * scale)
        parts[0] = parts[0] + share * state[...]
        return [window_tiles(parts[r], n * blocks[r], width) for r in range(4)]

    y = join(u_aq, ou_aq, oy_aq, 0, D)
    at_a = place(a_send, a_keep, 1, factor(u_aq, y, st_aq))
    y = join(u_akv, ou_akv, oy_akv, 2 * D, 3 * D)
    at_b = place(b_send, b_keep, 2, factor(u_akv, y, st_akv))

    y = join(u_gkv, ou_gkv, oy_gkv, 3 * D, 3 * D + KV)
    g_kv[...] = product(u_gkv[...], y) * scale
    small = [g_kv[pl.ds(pl.multiple_of(k * b, 8), k), :] for b in blocks]
    small[0] = small[0] + share * st_gkv[...]
    t_kv[:, :tokens] = ot_kv[...]
    t_kv[:, tokens:] = turned(other[:, 2 * D:3 * D])
    sums = four(product(
        left(t_kv), jnp.concatenate([gkv[...], theirs(3 * D, 3 * D + KV)], axis=0)
    ))
    h, e = n // 2, k // 2
    at_a = place(a_send, a_keep, 1, [[part[:h]] for part in sums], at_a)
    place(a_send, a_keep, 1, [[part[:e]] for part in small], at_a)
    at_b = place(b_send, b_keep, 2, [[part[h:]] for part in sums], at_b)
    place(b_send, b_keep, 2, [[part[e:]] for part in small], at_b)

    t_q[:, :tokens] = ot_q[...]
    t_q[:, tokens:] = turned(other[:, :D])
    sums = four(product(left(t_q), jnp.concatenate([gq[...], theirs(D, 2 * D)], axis=0)))
    sums = [plain_tiles(part) for part in sums]
    place(c_send, c_keep, 1, [tiles[:-1] for tiles in sums])
    y = join(u_gq, ou_gq, oy_gq, D, 2 * D)
    at_d = place(d_send, d_keep, 2, factor(u_gq, y, st_gq))
    place(d_send, d_keep, 2, [tiles[-1:] for tiles in sums], at_d)


def identity_rows(rows, extent, start):
    row = lax.broadcasted_iota(jnp.int32, (rows, extent), 0) + start
    column = lax.broadcasted_iota(jnp.int32, (rows, extent), 1)
    return row == column


def scaled_inverse_terms(matrix):
    extent = matrix.shape[0]
    on_diagonal = identity_rows(extent, extent, 0)
    trace = jnp.sum(jnp.where(on_diagonal, matrix, 0.0))
    damped = matrix + jnp.where(on_diagonal, DAMPING * trace / extent, 0.0)
    c = 1.0 / jnp.max(jnp.sum(jnp.abs(damped), axis=1))
    return c, c * damped


def halves(values):
    high = values.astype(BF16)
    return high, (values - high.astype(F32)).astype(BF16)


def times(values, high, low):
    v_high, v_low = halves(values)
    rows = values.shape[0]
    stacked = product(jnp.concatenate([v_high, v_low], axis=0), high)
    return stacked[:rows] + stacked[rows:] + product(v_high, low)


def piece_blocks(q, c):
    own = [2 * jnp.bitwise_xor(q, r) + c for r in range(4)]
    other = [2 * jnp.bitwise_xor(q, r) + (1 - c) for r in range(4)]
    return own + other


def assemble(pieces, blocks, n, width, extent, whole):
    tiles = width // LANES
    for piece, b in zip(pieces, blocks):
        parts = [piece[n * t:n * (t + 1), :] for t in range(tiles)]
        parts += [jnp.zeros((n, LANES), F32)] * (extent // LANES - tiles)
        turned = rolled(jnp.concatenate(parts, axis=1), n * b)
        whole[pl.ds(pl.multiple_of(n * b, 8), n), :] = turned
    windows = whole[...]

    def block_of(axis):
        shape = (extent, 1) if axis == 0 else (1, extent)
        index = lax.broadcasted_iota(jnp.int32, shape, axis)
        return sum([(index >= n * step).astype(jnp.int32) for step in range(1, 8)])

    apart = jnp.bitwise_and(block_of(1) - block_of(0), 7)
    matrix = jnp.where(apart <= 4, windows, windows.T)
    return matrix


def own_rows(ref, q, c, n):
    return ref[pl.ds(pl.multiple_of(n * (2 * q + c), 8), n), :]


def left_rows(c, rows, start, high, low):
    first = jnp.where(identity_rows(rows.shape[0], rows.shape[1], start), 2.0, 0.0) - rows
    second = times(first, high, low)
    third = 2.0 * second - times(second, high, low)
    return c * (2.0 * first - third)


def right_product(values, c, high, low):
    first = 2.0 * values - times(values, high, low)
    second = times(first, high, low)
    third = 2.0 * second - times(second, high, low)
    return c * (2.0 * first - third)


def left_kernel(n, width, pos, *refs):
    pieces, (new_ref, x_ref, whole, high_ref, low_ref) = refs[:8], refs[8:]
    q, c = pos[0], pos[1]
    extent = whole.shape[0]
    matrix = assemble(pieces, piece_blocks(q, c), n, width, extent, whole)
    whole[...] = matrix
    new_ref[...] = own_rows(whole, q, c, n)
    factor, scaled = scaled_inverse_terms(matrix)
    whole[...] = scaled
    high_ref[...], low_ref[...] = halves(scaled)
    x_ref[...] = left_rows(
        factor, own_rows(whole, q, c, n), n * (2 * q + c), high_ref[...], low_ref[...]
    )


def gradient_rows(main, rest, n):
    tiles = main.shape[0] // n
    parts = [main[n * t:n * (t + 1), :] for t in range(tiles)]
    return jnp.concatenate(parts + [rest[rest.shape[0] - n:, :]], axis=1)


def middle_kernel(n, pos, x_ref, *refs):
    mains, rests, (t_ref, high_ref, low_ref) = refs[:8], refs[8:16], refs[16:]
    q, c = pos[0], pos[1]
    for main, rest, b in zip(mains, rests, piece_blocks(q, c)):
        at = pl.ds(pl.multiple_of(n * b, 32), n)
        high_ref[at, :], low_ref[at, :] = halves(gradient_rows(main, rest, n))
    t_ref[...] = times(x_ref[...], high_ref[...], low_ref[...])


def right_kernel(n, width, pos, t_ref, main_own, *refs):
    pieces, (new_ref, step_ref, fit_ref, whole, high_ref, low_ref) = refs[:8], refs[8:]
    q, c = pos[0], pos[1]
    extent = whole.shape[0]
    matrix = assemble(pieces, piece_blocks(q, c), n, width, extent, whole)
    whole[...] = matrix
    new_ref[...] = own_rows(whole, q, c, n)
    factor, scaled = scaled_inverse_terms(matrix)
    high_ref[...], low_ref[...] = halves(scaled)
    step = right_product(t_ref[...], factor, high_ref[...], low_ref[...])
    step_ref[...] = step
    gradient = gradient_rows(main_own, pieces[0], n)
    fit_ref[...] = jnp.broadcast_to(jnp.sum(step * gradient), fit_ref.shape)


def keyval_kernel(n, k, width, pos, *refs):
    mates, pieces = refs[:8], refs[8:16]
    new_left, new_right, step_ref, fit_ref = refs[16:20]
    whole, high_ref, low_ref, grad_ref, g_ref = refs[20:]
    q, c = pos[0], pos[1]
    extent = whole.shape[0]
    blocks = piece_blocks(q, c)
    base = n * (width // LANES)
    h, e = n // 2, k // 2
    for mate, piece, b in zip(mates, pieces, blocks):
        for half, ref in ((0, mate), (1, piece)):
            at = pl.multiple_of(n * b + h * half, 8)
            grad_ref[pl.ds(at, h), :] = ref[base:base + h, :]
            at = pl.multiple_of(k * b + e * half, 8)
            g_ref[pl.ds(at, e), :] = ref[base + h:base + h + e, :]
    matrix = assemble(pieces, blocks, n, width, extent, whole)
    whole[...] = matrix
    new_left[...] = own_rows(whole, q, c, n)
    new_right[...] = own_rows(g_ref, q, c, k)
    factor, scaled = scaled_inverse_terms(matrix)
    whole[...] = scaled
    high_ref[...], low_ref[...] = halves(scaled)
    x_rows = left_rows(
        factor, own_rows(whole, q, c, n), n * (2 * q + c), high_ref[...], low_ref[...]
    )
    t_rows = times(x_rows, *halves(grad_ref[...]))
    factor, scaled = scaled_inverse_terms(g_ref[...])
    step = right_product(t_rows, factor, *halves(scaled))
    step_ref[...] = step
    fit_ref[...] = jnp.broadcast_to(jnp.sum(step * own_rows(grad_ref, q, c, n)), fit_ref.shape)


def update_kernel(fit_own, *refs):
    others, refs = refs[:7], refs[7:]
    (step_q, step_kv, weight_q, weight_kv, moment_q, moment_kv) = refs[:6]
    outs = refs[6:]
    total = fit_own[...]
    for other in others:
        total = total + other[...]
    fitness = total[:1, :1]
    scale = jnp.sqrt(TRUST_BOUND / (LEARNING_RATE * LEARNING_RATE * fitness))
    for step, weight, moment, at in (
        (step_q, weight_q, moment_q, 0), (step_kv, weight_kv, moment_kv, 1)
    ):
        fresh = MOMENTUM * moment[...] + scale * step[...]
        outs[2 + at][...] = fresh
        outs[at][...] = weight[...] - LEARNING_RATE * fresh


def call(kernel, outs, scratch, count, flops=0, scalars=1, kind=F32):
    vmem = pl.BlockSpec(memory_space=pltpu.VMEM)
    smem = pl.BlockSpec(memory_space=pltpu.SMEM)
    return pl.pallas_call(
        kernel,
        out_shape=[jax.ShapeDtypeStruct(shape, kind) for shape in outs],
        in_specs=[smem] * scalars + [vmem] * (count - scalars),
        out_specs=[vmem] * len(outs),
        scratch_shapes=[pltpu.VMEM(shape, kind) for shape, kind in scratch],
        compiler_params=pltpu.CompilerParams(vmem_limit_bytes=VMEM_LIMIT),
        cost_estimate=pl.CostEstimate(flops=flops, bytes_accessed=4_000_000, transcendentals=0),
    )


def flip(value, bit, axis="dp", size=8):
    return lax.ppermute(value, axis, [(i, i ^ bit) for i in range(size)])


def flip_plane(value, bit):
    return flip(value, bit, "group", 4)


X, Y = 2, 4


def in_order(*values):
    return lax.optimization_barrier(values)


def by_chip(first, own, near, across, far):
    pieces = {0: own, first: near, X + Y - first: across, X + Y: far}
    return [pieces[r] for r in (0, X, Y, X + Y)]


def reduce_and_spread(a, b, s, g):
    (a_send, a_keep), (b_send, b_keep), (s_send, s_keep), (g_send, g_keep) = a, b, s, g
    a_came, b_came = in_order(flip(a_send, X), flip(b_send, Y))
    a_next, b_next = a_keep[1] + a_came[1], b_keep[1] + b_came[1]
    a_own, b_own, s_send, g_send = in_order(
        a_keep[0] + a_came[0] + flip(a_next, Y),
        b_keep[0] + b_came[0] + flip(b_next, X),
        s_send, g_send,
    )
    a_own, b_own, s_came, g_came = in_order(
        a_own + flip_plane(a_own, 1), b_own + flip_plane(b_own, 2),
        flip(s_send, X), flip(g_send, Y),
    )
    s_next, g_next = s_keep[1] + s_came[1], g_keep[1] + g_came[1]
    a_own, b_own, s_own, g_own = in_order(
        a_own + flip_plane(a_own, 2), b_own + flip_plane(b_own, 1),
        s_keep[0] + s_came[0] + flip(s_next, Y),
        g_keep[0] + g_came[0] + flip(g_next, X),
    )
    a_near, a_across, b_near, b_across, s_own, g_own = in_order(
        flip(a_own, X), flip(a_own, Y), flip(b_own, Y), flip(b_own, X),
        s_own + flip_plane(s_own, 1), g_own + flip_plane(g_own, 2),
    )
    a_far, b_far, s_own, g_own = in_order(
        flip(a_across, X), flip(b_across, Y),
        s_own + flip_plane(s_own, 2), g_own + flip_plane(g_own, 1),
    )
    s_near, s_across, g_near, g_across = in_order(
        flip(s_own, X), flip(s_own, Y), flip(g_own, Y), flip(g_own, X),
    )
    s_far, g_far = flip(s_across, X), flip(g_across, Y)
    chunks = (
        by_chip(X, a_own, a_near, a_across, a_far),
        by_chip(Y, b_own, b_near, b_across, b_far),
        by_chip(X, s_own, s_near, s_across, s_far),
        by_chip(Y, g_own, g_near, g_across, g_far),
    )
    return [pieces + [flip(piece, 1) for piece in pieces] for pieces in chunks]


def fast_shards(
    act_query, grad_query, act_keyval, grad_keyval, sample_rows,
    state_aq, state_gq, state_akv, state_gkv,
    weight_query, weight_keyval, moment_query, moment_keyval,
):
    D, KV = act_query.shape[1], grad_keyval.shape[1]
    n, k = state_aq.shape[0], state_gkv.shape[0]
    tokens, samples = act_query.shape[0], sample_rows.shape[0]
    width = -(-5 * n // LANES) * LANES
    d = lax.axis_index("dp")
    pos = jnp.stack([d // 2, d % 2]).astype(jnp.int32)
    scale = (1.0 - BLEND_RATE) / (samples * 32)

    (mine,) = call(cast_kernel, [(tokens, 3 * D + KV)], [], 4, scalars=0)(
        act_query, grad_query, act_keyval, grad_keyval
    )
    rows_own = sample_rows.reshape(1, samples)
    rows_other = flip(rows_own, 1)
    other = flip(mine, 1)
    owns = call(
        own_kernel,
        [(samples, D)] * 3 + [(samples, KV)] + [(D, samples)] * 3 + [(KV, samples)]
        + [(D, tokens)] * 2,
        [], 5, 300_000_000, scalars=0, kind=BF16,
    )(rows_own, act_query, grad_query, act_keyval, grad_keyval)

    r_f = n * (width // LANES)
    r_kv = r_f + n // 2 + k // 2
    r_s = n * (D // LANES - 1)
    outs = []
    for rows in (r_kv, r_kv, r_s, r_f + n):
        outs += [(2, rows, LANES)] * 2
    grams = call(
        functools.partial(gram_kernel, n, k, width, scale),
        outs,
        [((D, 2 * samples), BF16)] * 3 + [((KV, 2 * samples), BF16)]
        + [((D, 2 * tokens), BF16)] * 2 + [((KV, KV), F32)],
        19,
        2_000_000_000,
    )(
        pos, rows_other, other, grad_query, grad_keyval, *owns,
        state_aq, state_gq, state_akv, state_gkv,
    )
    all_a, all_k, all_s, all_g = reduce_and_spread(grams[0:2], grams[2:4], grams[4:6], grams[6:8])

    square = [((D, D), F32), ((D, D), BF16), ((D, D), BF16)]
    fit = (8, LANES)
    new_aq, x_rows = call(
        functools.partial(left_kernel, n, width), [(n, D)] * 2, square, 9, 700_000_000
    )(pos, *all_a)
    new_akv, new_gkv, step_kv, fit_kv = call(
        functools.partial(keyval_kernel, n, k, width),
        [(n, D), (k, KV), (n, KV), fit],
        square + [((D, KV), F32), ((KV, KV), F32)],
        17,
        1_000_000_000,
    )(pos, *all_a, *all_k)
    (t_rows,) = call(
        functools.partial(middle_kernel, n), [(n, D)], square[1:], 18, 350_000_000
    )(pos, x_rows, *all_s, *all_g)
    new_gq, step_q, fit_q = call(
        functools.partial(right_kernel, n, width), [(n, D), (n, D), fit], square, 11, 1_000_000_000
    )(pos, t_rows, all_s[0], *all_g)

    part = fit_q + fit_kv
    weight_q, weight_kv, moment_q, moment_kv = call(
        update_kernel, [(n, D), (n, KV)] * 2, [], 14, scalars=0
    )(
        part, *[flip(part, bit) for bit in range(1, 8)], step_q, step_kv,
        weight_query, weight_keyval, moment_query, moment_keyval,
    )
    return (new_aq, new_gq, new_akv, new_gkv, weight_q, weight_kv, moment_q, moment_kv)


def from_root(value, axis, source):
    kept = jnp.where(lax.axis_index(axis) == source, value, 0).astype(value.dtype)
    return lax.psum(kept, axis)


def newton(damped):
    extent = damped.shape[0]
    identity = jnp.eye(extent, dtype=jnp.float32)
    inverse_norm = 1.0 / jnp.max(jnp.sum(jnp.abs(damped), axis=1))
    iterate = inverse_norm * (2.0 * identity - inverse_norm * damped)
    product = jnp.dot(damped, iterate, precision=PRECISE)
    iterate = jnp.dot(iterate, 2.0 * identity - product, precision=PRECISE)
    return iterate


def damped_inverse(factor):
    extent = factor.shape[0]
    identity = jnp.eye(extent, dtype=jnp.float32)
    return newton(factor + DAMPING * jnp.trace(factor) / extent * identity)


def precondition(left_inverse, gradient, right_inverse):
    return jnp.dot(
        jnp.dot(left_inverse, gradient, precision=PRECISE), right_inverse, precision=PRECISE
    )


def inner_rows(first_block, second_block):
    return lax.dot_general(
        first_block, second_block, (((0,), (0,)), ((), ())), preferred_element_type=jnp.float32
    )


def deliver(matrix, holder):
    return from_root(matrix, ("dp", "group"), holder)


def owner_step(left_factor, right_factor, gradient):
    return precondition(damped_inverse(left_factor), gradient, damped_inverse(right_factor))


def shards(
    act_query,
    grad_query,
    act_keyval,
    grad_keyval,
    sample_rows,
    state_aq,
    state_gq,
    state_akv,
    state_gkv,
    weight_query,
    weight_keyval,
    moment_query,
    moment_keyval,
):
    devices = lax.axis_size("dp") * lax.axis_size("group")
    total_samples = sample_rows.shape[0] * devices
    flat_index = lax.axis_index("dp") * lax.axis_size("group") + lax.axis_index("group")
    extent = state_aq.shape[0]
    start = lax.axis_index("dp") * extent

    def covariance(tokens_block):
        chosen = jnp.take(tokens_block, sample_rows, axis=0)
        return inner_rows(chosen, chosen)

    local_terms = (
        covariance(act_query),
        covariance(grad_query),
        covariance(act_keyval),
        covariance(grad_keyval),
        inner_rows(act_query, grad_query),
        inner_rows(act_keyval, grad_keyval),
    )
    shares = (
        lax.psum_scatter(local_terms[0], "dp", scatter_dimension=0, tiled=True),
        lax.psum_scatter(local_terms[1], "dp", scatter_dimension=0, tiled=True),
        lax.psum_scatter(local_terms[2], "dp", scatter_dimension=0, tiled=True),
        lax.psum_scatter(local_terms[3], "dp", scatter_dimension=0, tiled=True),
        lax.psum_scatter(local_terms[4], "dp", scatter_dimension=0, tiled=True),
        lax.psum_scatter(local_terms[5], "dp", scatter_dimension=0, tiled=True),
    )
    totals = lax.psum((shares[0], shares[1], shares[2], shares[3], shares[4], shares[5]), "group")
    cov_aq, cov_gq, cov_akv, cov_gkv, rows_q, rows_kv = totals
    new_aq = BLEND_RATE * state_aq + (1.0 - BLEND_RATE) * (cov_aq / total_samples)
    new_gq = BLEND_RATE * state_gq + (1.0 - BLEND_RATE) * (cov_gq / total_samples)
    new_akv = BLEND_RATE * state_akv + (1.0 - BLEND_RATE) * (cov_akv / total_samples)
    new_gkv = BLEND_RATE * state_gkv + (1.0 - BLEND_RATE) * (cov_gkv / total_samples)
    gathered = (
        lax.all_gather(new_aq, "dp", axis=0, tiled=True),
        lax.all_gather(new_gq, "dp", axis=0, tiled=True),
        lax.all_gather(new_akv, "dp", axis=0, tiled=True),
        lax.all_gather(new_gkv, "dp", axis=0, tiled=True),
        lax.all_gather(rows_q, "dp", axis=0, tiled=True),
        lax.all_gather(rows_kv, "dp", axis=0, tiled=True),
    )
    whole_aq, whole_gq, whole_akv, whole_gkv, whole_sum_q, whole_sum_kv = gathered
    holders = (0, 0, 1, 1)
    pairs = (
        (whole_aq, whole_gq, whole_sum_q, rows_q, holders[0], holders[1]),
        (whole_akv, whole_gkv, whole_sum_kv, rows_kv, holders[2], holders[3]),
    )
    step_rows = []
    fitness = jnp.zeros((), jnp.float32)
    for left_factor, right_factor, gradient, gradient_rows, left_holder, right_holder in pairs:
        whole_step = lax.cond(
            flat_index == left_holder,
            owner_step,
            lambda first, second, third: jnp.zeros_like(third),
            left_factor,
            right_factor,
            gradient,
        )
        whole_step = deliver(whole_step, left_holder)
        fitness = fitness + jnp.sum(whole_step * gradient)
        step_rows.append(lax.dynamic_slice_in_dim(whole_step, start, extent, 0))
    scale = jnp.sqrt(TRUST_BOUND / (LEARNING_RATE * LEARNING_RATE * fitness))
    moment_q = MOMENTUM * moment_query + scale * step_rows[0]
    moment_kv = MOMENTUM * moment_keyval + scale * step_rows[1]
    weight_q = weight_query - LEARNING_RATE * moment_q
    weight_kv = weight_keyval - LEARNING_RATE * moment_kv
    return (new_aq, new_gq, new_akv, new_gkv, weight_q, weight_kv, moment_q, moment_kv)


def solution(mesh):
    placed = (
        P(("dp", "group"), None),
        P(("dp", "group"), None),
        P(("dp", "group"), None),
        P(("dp", "group"), None),
        P(("dp", "group")),
        P("dp", None),
        P("dp", None),
        P("dp", None),
        P("dp", None),
        P("dp", None),
        P("dp", None),
        P("dp", None),
        P("dp", None),
    )
    plane = mesh.shape["dp"] == 8 and mesh.shape["group"] == 4
    return jax.shard_map(
        fast_shards if plane else shards,
        mesh=mesh,
        in_specs=placed,
        out_specs=(
            P("dp", None),
            P("dp", None),
            P("dp", None),
            P("dp", None),
            P("dp", None),
            P("dp", None),
            P("dp", None),
            P("dp", None),
        ),
        check_vma=False,
    )
```

```python
import functools

import jax
import jax.numpy as jnp
from jax import lax
from jax.experimental import pallas as pl
from jax.experimental.pallas import tpu as pltpu
from jax.sharding import PartitionSpec as P

PRECISE = lax.Precision.HIGHEST
BLEND_RATE = 0.8
DAMPING = 0.05
MOMENTUM = 0.9
LEARNING_RATE = 0.001
TRUST_BOUND = 0.5
LANES = 128
F32 = jnp.float32
BF16 = jnp.bfloat16
VMEM_LIMIT = 28 * 1024 * 1024


def rolled(block, shift):
    return pltpu.roll(block, shift, 1)


def window_tiles(block, start, width):
    extent = block.shape[1]
    shift = lax.rem(extent - start, extent)
    turned = rolled(block, shift)
    return [turned[:, LANES * t:LANES * (t + 1)] for t in range(width // LANES)]


def plain_tiles(block):
    return [block[:, LANES * t:LANES * (t + 1)] for t in range(block.shape[1] // LANES)]


def write_tiles(ref, lead, tiles, at=0):
    for tile in tiles:
        ref[lead, at:at + tile.shape[0], :] = tile
        at += tile.shape[0]
    return at


def product(first, second):
    return lax.dot_general(
        first, second, (((1,), (0,)), ((), ())), preferred_element_type=F32
    )


def cast_kernel(rows, aq, gq, akv, gkv, out):
    at, tokens = 0, aq.shape[0]
    for ref in (aq, gq, akv, gkv):
        out[:tokens, at:at + ref.shape[1]] = ref[...].astype(F32)
        at += ref.shape[1]
    out[tokens:, :] = jnp.zeros((out.shape[0] - tokens, at), F32)
    out[tokens:tokens + 1, :rows.shape[1]] = rows[...].astype(F32)


def picker(all_tokens, tokens, samples):
    rows = all_tokens[tokens:tokens + 1, :samples].astype(jnp.int32)
    token = lax.broadcasted_iota(jnp.int32, (tokens, samples), 0)
    return (token == rows).astype(F32).T.astype(BF16)


def turned(values):
    return values.astype(F32).T.astype(BF16)


def own_kernel(tokens, samples, D, mine, y_aq, y_gq, y_akv, y_gkv, u_aq, u_gq, u_akv, u_gkv, t_q, t_kv):
    pick = picker(mine, tokens, samples)
    at = 0
    for y, u in ((y_aq, u_aq), (y_gq, u_gq), (y_akv, u_akv), (y_gkv, u_gkv)):
        chosen = product(pick, mine[:tokens, at:at + y.shape[1]].astype(BF16))
        y[...] = chosen.astype(BF16)
        u[...] = chosen.T.astype(BF16)
        at += y.shape[1]
    t_q[...] = turned(mine[:tokens, :D])
    t_kv[...] = turned(mine[:tokens, 2 * D:3 * D])


def roles(q, c):
    return [2 * chip + c for chip in (q, q ^ (1 + c), q ^ (2 - c), q ^ 3)]


def join(u, other, pick, own_u, own_y, lo, hi):
    samples, tokens = pick.shape
    chosen = product(pick, other[:tokens, lo:hi].astype(BF16))
    u[:, :samples] = own_u[...]
    u[:, samples:] = chosen.T.astype(BF16)
    return jnp.concatenate([own_y[...], chosen.astype(BF16)], axis=0)


def left_blocks(ref, n, blocks):
    parts = [ref[pl.ds(pl.multiple_of(n * b, 32), n), :] for b in blocks]
    return jnp.concatenate(parts, axis=0)


def four(values, n):
    return [values[n * r:n * (r + 1)] for r in range(4)]


def place(send, keep, tiles, at=0):
    write_tiles(send, 0, tiles[1], at)
    write_tiles(send, 1, tiles[3], at)
    write_tiles(keep, 0, tiles[0], at)
    return write_tiles(keep, 1, tiles[2], at)


def factor_tiles(u, y, state, n, blocks, width, scale):
    parts = four(product(left_blocks(u, n, blocks), y) * scale, n)
    parts[0] = parts[0] + (BLEND_RATE / 4.0) * state[...]
    return [window_tiles(part, n * b, width) for part, b in zip(parts, blocks)]


def first_kernel(
    n, k, width, scale,
    pos, mine, other, y_aq, y_akv, y_gkv, o_aq, o_akv, o_gkv, o_kv, st_aq, st_akv, st_gkv,
    send, keep, u_aq, u_akv, u_gkv, t_kv, g_kv,
):
    tokens, samples = o_kv.shape[1], o_aq.shape[1]
    D, KV = y_aq.shape[1], y_gkv.shape[1]
    blocks = roles(pos[0], pos[1])
    pick = picker(other, tokens, samples)
    y = join(u_aq, other, pick, o_aq, y_aq, 0, D)
    at = place(send, keep, factor_tiles(u_aq, y, st_aq, n, blocks, width, scale))
    y = join(u_akv, other, pick, o_akv, y_akv, 2 * D, 3 * D)
    at = place(send, keep, factor_tiles(u_akv, y, st_akv, n, blocks, width, scale), at)
    t_kv[:, :tokens] = o_kv[...]
    t_kv[:, tokens:] = turned(other[:tokens, 2 * D:3 * D])
    ends = [ref[:tokens, 3 * D:].astype(BF16) for ref in (mine, other)]
    sums = product(left_blocks(t_kv, n, blocks), jnp.concatenate(ends, axis=0))
    at = place(send, keep, [[part] for part in four(sums, n)], at)
    y = join(u_gkv, other, pick, o_gkv, y_gkv, 3 * D, 3 * D + KV)
    g_kv[...] = product(u_gkv[...], y) * scale
    small = [g_kv[pl.ds(pl.multiple_of(k * b, 8), k), :] for b in blocks]
    small[0] = small[0] + (BLEND_RATE / 4.0) * st_gkv[...]
    place(send, keep, [[part] for part in small], at)


def second_kernel(
    n, width, scale,
    pos, mine, other, y_gq, o_gq, o_q, st_gq, send, keep, u_gq, t_q,
):
    tokens, samples = o_q.shape[1], o_gq.shape[1]
    D = y_gq.shape[1]
    blocks = roles(pos[0], pos[1])
    pick = picker(other, tokens, samples)
    t_q[:, :tokens] = o_q[...]
    t_q[:, tokens:] = turned(other[:tokens, :D])
    ends = [ref[:tokens, D:2 * D].astype(BF16) for ref in (mine, other)]
    sums = four(product(left_blocks(t_q, n, blocks), jnp.concatenate(ends, axis=0)), n)
    at = place(send, keep, [plain_tiles(part) for part in sums])
    y = join(u_gq, other, pick, o_gq, y_gq, D, 2 * D)
    place(send, keep, factor_tiles(u_gq, y, st_gq, n, blocks, width, scale), at)


def identity_rows(rows, extent, start):
    row = lax.broadcasted_iota(jnp.int32, (rows, extent), 0) + start
    column = lax.broadcasted_iota(jnp.int32, (rows, extent), 1)
    return row == column


def scaled_inverse_terms(matrix):
    extent = matrix.shape[0]
    on_diagonal = identity_rows(extent, extent, 0)
    trace = jnp.sum(jnp.where(on_diagonal, matrix, 0.0))
    damped = matrix + jnp.where(on_diagonal, DAMPING * trace / extent, 0.0)
    c = 1.0 / jnp.max(jnp.sum(jnp.abs(damped), axis=1))
    return c, c * damped


def halves(values):
    high = values.astype(BF16)
    return high, (values - high.astype(F32)).astype(BF16)


def times(values, high, low):
    v_high, v_low = halves(values)
    rows = values.shape[0]
    stacked = product(jnp.concatenate([v_high, v_low], axis=0), high)
    return stacked[:rows] + stacked[rows:] + product(v_high, low)


def pieces_of(stacks, q, c):
    near, far = (roles(q, parity) for parity in (c, 1 - c))
    order = [(0, 0, 0), (0, 1, 2), (1, 0, 1), (1, 1, 3)]
    found = []
    for stack, blocks in ((stacks[:2], near), (stacks[2:], far)):
        found += [(stack[which].at[lead], blocks[role]) for which, lead, role in order]
    return found


def assemble(pieces, at, n, width, extent, whole):
    tiles = width // LANES
    for piece, b in pieces:
        parts = [piece[at + n * t:at + n * (t + 1), :] for t in range(tiles)]
        parts += [jnp.zeros((n, LANES), F32)] * (extent // LANES - tiles)
        turned = rolled(jnp.concatenate(parts, axis=1), n * b)
        whole[pl.ds(pl.multiple_of(n * b, 8), n), :] = turned
    windows = whole[...]

    def block_of(axis):
        shape = (extent, 1) if axis == 0 else (1, extent)
        index = lax.broadcasted_iota(jnp.int32, shape, axis)
        return sum([(index >= n * step).astype(jnp.int32) for step in range(1, 8)])

    apart = jnp.bitwise_and(block_of(1) - block_of(0), 7)
    matrix = jnp.where(apart <= 4, windows, windows.T)
    return matrix


def own_rows(ref, q, c, n):
    return ref[pl.ds(pl.multiple_of(n * (2 * q + c), 8), n), :]


def parity_rows(ref, c, n):
    parts = [ref[pl.ds(pl.multiple_of(n * (2 * j + c), 8), n), :] for j in range(4)]
    return jnp.concatenate(parts, axis=0)


def identity_parity(extent, c, n):
    parts = [identity_rows(n, extent, n * (2 * j + c)) for j in range(4)]
    return jnp.concatenate(parts, axis=0)


def left_rows(c, rows, identity, high, low):
    first = jnp.where(identity, 2.0, 0.0) - rows
    second = times(first, high, low)
    third = 2.0 * second - times(second, high, low)
    return c * (2.0 * first - third)


def right_product(values, c, high, low):
    first = 2.0 * values - times(values, high, low)
    second = times(first, high, low)
    third = 2.0 * second - times(second, high, low)
    return c * (2.0 * first - third)


def left_inverse(matrix, c, n, whole, high_ref, low_ref):
    factor, scaled = scaled_inverse_terms(matrix)
    whole[...] = scaled
    high_ref[...], low_ref[...] = halves(scaled)
    return left_rows(
        factor, parity_rows(whole, c, n), identity_parity(whole.shape[0], c, n),
        high_ref[...], low_ref[...],
    )


def left_kernel(n, width, pos, *refs):
    stacks, (new_ref, x_ref, whole, high_ref, low_ref) = refs[:4], refs[4:]
    q, c = pos[0], pos[1]
    matrix = assemble(pieces_of(stacks, q, c), 0, n, width, whole.shape[0], whole)
    whole[...] = matrix
    new_ref[...] = own_rows(whole, q, c, n)
    x_ref[...] = left_inverse(matrix, c, n, whole, high_ref, low_ref)


def query_kernel(n, width, pos, x_ref, *refs):
    stacks, (new_ref, step_ref, fit_ref) = refs[:4], refs[4:7]
    whole, high_ref, low_ref, s_ref, s_high, s_low, t_ref = refs[7:]
    q, c = pos[0], pos[1]
    extent = whole.shape[0]
    tiles = extent // LANES
    pieces = pieces_of(stacks, q, c)
    for piece, b in pieces:
        rows = jnp.concatenate([piece[n * t:n * (t + 1), :] for t in range(tiles)], axis=1)
        at = pl.ds(pl.multiple_of(n * b, 32), n)
        s_ref[at, :] = rows
        s_high[at, :], s_low[at, :] = halves(rows)
    t_ref[...] = times(x_ref[...], s_high[...], s_low[...])
    matrix = assemble(pieces, n * tiles, n, width, extent, whole)
    whole[...] = matrix
    new_ref[...] = own_rows(whole, q, c, n)
    factor, scaled = scaled_inverse_terms(matrix)
    high_ref[...], low_ref[...] = halves(scaled)
    step = right_product(t_ref[...], factor, high_ref[...], low_ref[...])
    t_ref[...] = step
    step_ref[...] = t_ref[pl.ds(pl.multiple_of(n * q, 8), n), :]
    fit_ref[...] = jnp.broadcast_to(jnp.sum(step * parity_rows(s_ref, c, n)), fit_ref.shape)


def keyval_kernel(n, k, width, pos, *refs):
    stacks, (new_left, new_right, step_ref, fit_ref) = refs[:4], refs[4:8]
    whole, high_ref, low_ref, grad_ref, g_ref, t_ref = refs[8:]
    q, c = pos[0], pos[1]
    pieces = pieces_of(stacks, q, c)
    size = n * (width // LANES)
    for piece, b in pieces:
        at = 2 * size
        grad_ref[pl.ds(pl.multiple_of(n * b, 8), n), :] = piece[at:at + n, :]
        g_ref[pl.ds(pl.multiple_of(k * b, 8), k), :] = piece[at + n:at + n + k, :]
    matrix = assemble(pieces, size, n, width, whole.shape[0], whole)
    whole[...] = matrix
    new_left[...] = own_rows(whole, q, c, n)
    new_right[...] = own_rows(g_ref, q, c, k)
    x_rows = left_inverse(matrix, c, n, whole, high_ref, low_ref)
    t_rows = times(x_rows, *halves(grad_ref[...]))
    factor, scaled = scaled_inverse_terms(g_ref[...])
    step = right_product(t_rows, factor, *halves(scaled))
    t_ref[...] = step
    step_ref[...] = t_ref[pl.ds(pl.multiple_of(n * q, 8), n), :]
    fit_ref[...] = jnp.broadcast_to(jnp.sum(step * parity_rows(grad_ref, c, n)), fit_ref.shape)


def update_kernel(fit_own, fit_other, *refs):
    (step_q, step_kv, weight_q, weight_kv, moment_q, moment_kv) = refs[:6]
    outs = refs[6:]
    fitness = (fit_own[...] + fit_other[...])[:1, :1]
    scale = jnp.sqrt(TRUST_BOUND / (LEARNING_RATE * LEARNING_RATE * fitness))
    for step, weight, moment, at in (
        (step_q, weight_q, moment_q, 0), (step_kv, weight_kv, moment_kv, 1)
    ):
        fresh = MOMENTUM * moment[...] + scale * step[...]
        outs[2 + at][...] = fresh
        outs[at][...] = weight[...] - LEARNING_RATE * fresh


def call(kernel, outs, scratch, count, flops=0, scalars=1, kind=F32):
    vmem = pl.BlockSpec(memory_space=pltpu.VMEM)
    smem = pl.BlockSpec(memory_space=pltpu.SMEM)
    return pl.pallas_call(
        kernel,
        out_shape=[jax.ShapeDtypeStruct(shape, kind) for shape in outs],
        in_specs=[smem] * scalars + [vmem] * (count - scalars),
        out_specs=[vmem] * len(outs),
        scratch_shapes=[pltpu.VMEM(shape, kind) for shape, kind in scratch],
        compiler_params=pltpu.CompilerParams(vmem_limit_bytes=VMEM_LIMIT),
        cost_estimate=pl.CostEstimate(flops=flops, bytes_accessed=4_000_000, transcendentals=0),
    )


def core_flip(value):
    return lax.ppermute(value, "dp", [(i, i ^ 1) for i in range(8)])


def first_hop(value):
    return lax.ppermute(value, "dp", [(i, i ^ (4 if i & 1 else 2)) for i in range(8)])


def second_hop(value):
    return lax.ppermute(value, "dp", [(i, i ^ (2 if i & 1 else 4)) for i in range(8)])


def plane_flip(value, bit):
    return lax.ppermute(value, "group", [(i, i ^ bit) for i in range(4)])


def after(value, *others):
    return lax.optimization_barrier((value,) + others)[0]


def plane_halves(piece):
    half = piece.shape[0] // 2
    even = lax.axis_index("group") % 2 == 0
    low, high = piece[:half], piece[half:]
    return jnp.where(even, low, high), jnp.where(even, high, low)


def plane_whole(mine, theirs):
    even = lax.axis_index("group") % 2 == 0
    return jnp.concatenate(
        [jnp.where(even, mine, theirs), jnp.where(even, theirs, mine)], axis=0
    )


def fast_shards(
    act_query, grad_query, act_keyval, grad_keyval, sample_rows,
    state_aq, state_gq, state_akv, state_gkv,
    weight_query, weight_keyval, moment_query, moment_keyval,
):
    D, KV = act_query.shape[1], grad_keyval.shape[1]
    n, k = state_aq.shape[0], state_gkv.shape[0]
    tokens, samples = act_query.shape[0], sample_rows.shape[0]
    width = -(-5 * n // LANES) * LANES
    d = lax.axis_index("dp")
    pos = jnp.stack([d // 2, d % 2]).astype(jnp.int32)
    scale = (1.0 - BLEND_RATE) / (samples * 32)

    (mine,) = call(cast_kernel, [(tokens + 8, 3 * D + KV)], [], 5, scalars=0)(
        sample_rows.reshape(1, samples), act_query, grad_query, act_keyval, grad_keyval
    )
    other = core_flip(mine)
    y_aq, y_gq, y_akv, y_gkv, u_aq, u_gq, u_akv, u_gkv, t_q, t_kv = call(
        functools.partial(own_kernel, tokens, samples, D),
        [(samples, D)] * 3 + [(samples, KV)] + [(D, samples)] * 3 + [(KV, samples)]
        + [(D, tokens)] * 2,
        [], 1, 300_000_000, scalars=0, kind=BF16,
    )(mine)

    r_f = n * (width // LANES)
    r_a, r_b = 2 * r_f + n + k, n * (D // LANES) + r_f
    both = (D, 2 * samples)
    a_send, a_keep = call(
        functools.partial(first_kernel, n, k, width, scale), [(2, r_a, LANES)] * 2,
        [(both, BF16)] * 2 + [((KV, 2 * samples), BF16), ((D, 2 * tokens), BF16), ((KV, KV), F32)],
        13, 700_000_000,
    )(
        pos, mine, other, y_aq, y_akv, y_gkv, u_aq, u_akv, u_gkv, t_kv,
        state_aq, state_akv, state_gkv,
    )
    b_send, b_keep = call(
        functools.partial(second_kernel, n, width, scale), [(2, r_b, LANES)] * 2,
        [(both, BF16), ((D, 2 * tokens), BF16)], 7, 700_000_000,
    )(pos, mine, other, y_gq, u_gq, t_q, state_gq)

    a_came = first_hop(a_send)
    a_own = a_keep[0] + a_came[0] + second_hop(a_keep[1] + a_came[1])
    b_came = first_hop(after(b_send, a_own))
    a_mine, a_theirs = plane_halves(a_own)
    a_mine = a_mine + plane_flip(a_theirs, 1)
    a_mine = a_mine + plane_flip(a_mine, 2)
    b_own = b_keep[0] + b_came[0] + second_hop(b_keep[1] + b_came[1])
    a_own = plane_whole(a_mine, plane_flip(a_mine, 1))
    b_mine, b_theirs = plane_halves(b_own)
    a_across = second_hop(after(a_own, b_own))
    b_mine = b_mine + plane_flip(b_theirs, 1)
    b_came = plane_flip(b_mine, 2)
    a_near = jnp.stack([a_own, a_across])
    a_far = first_hop(a_near)
    b_mine = b_mine + b_came
    b_own = plane_whole(b_mine, plane_flip(b_mine, 1))
    all_a = (a_near, a_far, core_flip(a_near), core_flip(a_far))
    b_own = after(b_own, *all_a)
    b_across = second_hop(b_own)

    half = (4 * n, D)
    square = [((D, D), F32), ((D, D), BF16), ((D, D), BF16)]
    fit = (8, LANES)
    new_aq, x_rows = call(
        functools.partial(left_kernel, n, width), [(n, D), half], square, 5, 2_000_000_000
    )(pos, *all_a)
    b_near = after(jnp.stack([b_own, b_across]), x_rows)
    b_far = first_hop(b_near)
    b_near_other = core_flip(b_near)
    new_akv, new_gkv, step_kv, fit_kv = call(
        functools.partial(keyval_kernel, n, k, width),
        [(n, D), (k, KV), (n, KV), fit],
        square + [((D, KV), F32), ((KV, KV), F32), ((4 * n, KV), F32)],
        5,
        3_000_000_000,
    )(pos, *all_a)
    b_far_other = core_flip(after(b_far, fit_kv))
    new_gq, step_q, fit_q = call(
        functools.partial(query_kernel, n, width), [(n, D), (n, D), fit],
        square + [((D, D), F32), ((D, D), BF16), ((D, D), BF16), (half, F32)], 6, 5_000_000_000,
    )(pos, x_rows, b_near, b_far, b_near_other, b_far_other)

    part = fit_q + fit_kv
    weight_q, weight_kv, moment_q, moment_kv = call(
        update_kernel, [(n, D), (n, KV)] * 2, [], 8, scalars=0
    )(
        part, core_flip(part), step_q, step_kv,
        weight_query, weight_keyval, moment_query, moment_keyval,
    )
    return (new_aq, new_gq, new_akv, new_gkv, weight_q, weight_kv, moment_q, moment_kv)


def from_root(value, axis, source):
    kept = jnp.where(lax.axis_index(axis) == source, value, 0).astype(value.dtype)
    return lax.psum(kept, axis)


def newton(damped):
    extent = damped.shape[0]
    identity = jnp.eye(extent, dtype=jnp.float32)
    inverse_norm = 1.0 / jnp.max(jnp.sum(jnp.abs(damped), axis=1))
    iterate = inverse_norm * (2.0 * identity - inverse_norm * damped)
    product = jnp.dot(damped, iterate, precision=PRECISE)
    iterate = jnp.dot(iterate, 2.0 * identity - product, precision=PRECISE)
    return iterate


def damped_inverse(factor):
    extent = factor.shape[0]
    identity = jnp.eye(extent, dtype=jnp.float32)
    return newton(factor + DAMPING * jnp.trace(factor) / extent * identity)


def precondition(left_inverse, gradient, right_inverse):
    return jnp.dot(
        jnp.dot(left_inverse, gradient, precision=PRECISE), right_inverse, precision=PRECISE
    )


def inner_rows(first_block, second_block):
    return lax.dot_general(
        first_block, second_block, (((0,), (0,)), ((), ())), preferred_element_type=jnp.float32
    )


def deliver(matrix, holder):
    return from_root(matrix, ("dp", "group"), holder)


def owner_step(left_factor, right_factor, gradient):
    return precondition(damped_inverse(left_factor), gradient, damped_inverse(right_factor))


def shards(
    act_query,
    grad_query,
    act_keyval,
    grad_keyval,
    sample_rows,
    state_aq,
    state_gq,
    state_akv,
    state_gkv,
    weight_query,
    weight_keyval,
    moment_query,
    moment_keyval,
):
    devices = lax.axis_size("dp") * lax.axis_size("group")
    total_samples = sample_rows.shape[0] * devices
    flat_index = lax.axis_index("dp") * lax.axis_size("group") + lax.axis_index("group")
    extent = state_aq.shape[0]
    start = lax.axis_index("dp") * extent

    def covariance(tokens_block):
        chosen = jnp.take(tokens_block, sample_rows, axis=0)
        return inner_rows(chosen, chosen)

    local_terms = (
        covariance(act_query),
        covariance(grad_query),
        covariance(act_keyval),
        covariance(grad_keyval),
        inner_rows(act_query, grad_query),
        inner_rows(act_keyval, grad_keyval),
    )
    shares = (
        lax.psum_scatter(local_terms[0], "dp", scatter_dimension=0, tiled=True),
        lax.psum_scatter(local_terms[1], "dp", scatter_dimension=0, tiled=True),
        lax.psum_scatter(local_terms[2], "dp", scatter_dimension=0, tiled=True),
        lax.psum_scatter(local_terms[3], "dp", scatter_dimension=0, tiled=True),
        lax.psum_scatter(local_terms[4], "dp", scatter_dimension=0, tiled=True),
        lax.psum_scatter(local_terms[5], "dp", scatter_dimension=0, tiled=True),
    )
    totals = lax.psum((shares[0], shares[1], shares[2], shares[3], shares[4], shares[5]), "group")
    cov_aq, cov_gq, cov_akv, cov_gkv, rows_q, rows_kv = totals
    new_aq = BLEND_RATE * state_aq + (1.0 - BLEND_RATE) * (cov_aq / total_samples)
    new_gq = BLEND_RATE * state_gq + (1.0 - BLEND_RATE) * (cov_gq / total_samples)
    new_akv = BLEND_RATE * state_akv + (1.0 - BLEND_RATE) * (cov_akv / total_samples)
    new_gkv = BLEND_RATE * state_gkv + (1.0 - BLEND_RATE) * (cov_gkv / total_samples)
    gathered = (
        lax.all_gather(new_aq, "dp", axis=0, tiled=True),
        lax.all_gather(new_gq, "dp", axis=0, tiled=True),
        lax.all_gather(new_akv, "dp", axis=0, tiled=True),
        lax.all_gather(new_gkv, "dp", axis=0, tiled=True),
        lax.all_gather(rows_q, "dp", axis=0, tiled=True),
        lax.all_gather(rows_kv, "dp", axis=0, tiled=True),
    )
    whole_aq, whole_gq, whole_akv, whole_gkv, whole_sum_q, whole_sum_kv = gathered
    holders = (0, 0, 1, 1)
    pairs = (
        (whole_aq, whole_gq, whole_sum_q, rows_q, holders[0], holders[1]),
        (whole_akv, whole_gkv, whole_sum_kv, rows_kv, holders[2], holders[3]),
    )
    step_rows = []
    fitness = jnp.zeros((), jnp.float32)
    for left_factor, right_factor, gradient, gradient_rows, left_holder, right_holder in pairs:
        whole_step = lax.cond(
            flat_index == left_holder,
            owner_step,
            lambda first, second, third: jnp.zeros_like(third),
            left_factor,
            right_factor,
            gradient,
        )
        whole_step = deliver(whole_step, left_holder)
        fitness = fitness + jnp.sum(whole_step * gradient)
        step_rows.append(lax.dynamic_slice_in_dim(whole_step, start, extent, 0))
    scale = jnp.sqrt(TRUST_BOUND / (LEARNING_RATE * LEARNING_RATE * fitness))
    moment_q = MOMENTUM * moment_query + scale * step_rows[0]
    moment_kv = MOMENTUM * moment_keyval + scale * step_rows[1]
    weight_q = weight_query - LEARNING_RATE * moment_q
    weight_kv = weight_keyval - LEARNING_RATE * moment_kv
    return (new_aq, new_gq, new_akv, new_gkv, weight_q, weight_kv, moment_q, moment_kv)


def solution(mesh):
    placed = (
        P(("dp", "group"), None),
        P(("dp", "group"), None),
        P(("dp", "group"), None),
        P(("dp", "group"), None),
        P(("dp", "group")),
        P("dp", None),
        P("dp", None),
        P("dp", None),
        P("dp", None),
        P("dp", None),
        P("dp", None),
        P("dp", None),
        P("dp", None),
    )
    plane = mesh.shape["dp"] == 8 and mesh.shape["group"] == 4
    return jax.shard_map(
        fast_shards if plane else shards,
        mesh=mesh,
        in_specs=placed,
        out_specs=(
            P("dp", None),
            P("dp", None),
            P("dp", None),
            P("dp", None),
            P("dp", None),
            P("dp", None),
            P("dp", None),
            P("dp", None),
        ),
        check_vma=False,
    )
```

```python
import functools

import jax
import jax.numpy as jnp
from jax import lax
from jax.experimental import pallas as pl
from jax.experimental.pallas import tpu as pltpu
from jax.sharding import PartitionSpec as P

PRECISE = lax.Precision.HIGHEST
BLEND_RATE = 0.8
DAMPING = 0.05
MOMENTUM = 0.9
LEARNING_RATE = 0.001
TRUST_BOUND = 0.5
LANES = 128
F32 = jnp.float32
BF16 = jnp.bfloat16
VMEM_LIMIT = 28 * 1024 * 1024


def rolled(block, shift):
    return pltpu.roll(block, shift, 1)


def window_tiles(block, start, width):
    extent = block.shape[1]
    shift = lax.rem(extent - start, extent)
    turned = rolled(block, shift)
    return [turned[:, LANES * t:LANES * (t + 1)] for t in range(width // LANES)]


def plain_tiles(block):
    return [block[:, LANES * t:LANES * (t + 1)] for t in range(block.shape[1] // LANES)]


def write_tiles(ref, lead, tiles, at=0):
    for tile in tiles:
        ref[lead, at:at + tile.shape[0], :] = tile
        at += tile.shape[0]
    return at


def product(first, second):
    return lax.dot_general(
        first, second, (((1,), (0,)), ((), ())), preferred_element_type=F32
    )


def cast_kernel(rows, aq, gq, akv, gkv, out):
    at, tokens = 0, aq.shape[0]
    for ref in (aq, gq, akv, gkv):
        out[:tokens, at:at + ref.shape[1]] = ref[...].astype(F32)
        at += ref.shape[1]
    out[tokens:, :] = jnp.zeros((out.shape[0] - tokens, at), F32)
    out[tokens:tokens + 1, :rows.shape[1]] = rows[...].astype(F32)


def picker(all_tokens, tokens, samples):
    rows = all_tokens[tokens:tokens + 1, :samples].astype(jnp.int32)
    token = lax.broadcasted_iota(jnp.int32, (tokens, samples), 0)
    return (token == rows).astype(F32).T.astype(BF16)


def turned(values):
    return values.astype(F32).T.astype(BF16)


def own_kernel(tokens, samples, D, mine, y_aq, y_gq, y_akv, y_gkv, u_aq, u_gq, u_akv, u_gkv, t_q, t_kv):
    pick = picker(mine, tokens, samples)
    at = 0
    for y, u in ((y_aq, u_aq), (y_gq, u_gq), (y_akv, u_akv), (y_gkv, u_gkv)):
        chosen = product(pick, mine[:tokens, at:at + y.shape[1]].astype(BF16))
        y[...] = chosen.astype(BF16)
        u[...] = chosen.T.astype(BF16)
        at += y.shape[1]
    t_q[...] = turned(mine[:tokens, :D])
    t_kv[...] = turned(mine[:tokens, 2 * D:3 * D])


def roles(q, c):
    return [2 * chip + c for chip in (q, q ^ (1 + c), q ^ (2 - c), q ^ 3)]


def join(u, other, pick, own_u, own_y, lo, hi):
    samples, tokens = pick.shape
    chosen = product(pick, other[:tokens, lo:hi].astype(BF16))
    u[:, :samples] = own_u[...]
    u[:, samples:] = chosen.T.astype(BF16)
    return jnp.concatenate([own_y[...], chosen.astype(BF16)], axis=0)


def left_blocks(ref, n, blocks):
    parts = [ref[pl.ds(pl.multiple_of(n * b, 32), n), :] for b in blocks]
    return jnp.concatenate(parts, axis=0)


def four(values, n):
    return [values[n * r:n * (r + 1)] for r in range(4)]


def place(send, keep, tiles, at=0):
    write_tiles(send, 0, tiles[1], at)
    write_tiles(send, 1, tiles[3], at)
    write_tiles(keep, 0, tiles[0], at)
    return write_tiles(keep, 1, tiles[2], at)


def factor_tiles(u, y, state, n, blocks, width, scale):
    parts = four(product(left_blocks(u, n, blocks), y) * scale, n)
    parts[0] = parts[0] + (BLEND_RATE / 4.0) * state[...]
    return [window_tiles(part, n * b, width) for part, b in zip(parts, blocks)]


def factor_kernel(n, width, scale, lo, pos, other, y, o, state, send, keep, u):
    D, samples = y.shape[1], y.shape[0]
    tokens = other.shape[0] - 8
    blocks = roles(pos[0], pos[1])
    chosen = join(u, other, picker(other, tokens, samples), o, y, lo, lo + D)
    place(send, keep, factor_tiles(u, chosen, state, n, blocks, width, scale))


def gradient_kernel(n, pos, mine, other, o_q, send, keep, t_q):
    D, tokens = o_q.shape
    t_q[:, :tokens] = o_q[...]
    t_q[:, tokens:] = turned(other[:tokens, :D])
    ends = [ref[:tokens, D:2 * D].astype(BF16) for ref in (mine, other)]
    sums = product(left_blocks(t_q, n, roles(pos[0], pos[1])), jnp.concatenate(ends, axis=0))
    place(send, keep, [plain_tiles(part) for part in four(sums, n)])


def keyval_sums_kernel(
    n, k, width, scale,
    pos, mine, other, y_akv, y_gkv, o_akv, o_gkv, o_kv, st_akv, st_gkv,
    send, keep, u_akv, u_gkv, t_kv, g_kv,
):
    tokens, samples = o_kv.shape[1], o_akv.shape[1]
    D, KV = y_akv.shape[1], y_gkv.shape[1]
    blocks = roles(pos[0], pos[1])
    pick = picker(other, tokens, samples)
    y = join(u_akv, other, pick, o_akv, y_akv, 2 * D, 3 * D)
    at = place(send, keep, factor_tiles(u_akv, y, st_akv, n, blocks, width, scale))
    t_kv[:, :tokens] = o_kv[...]
    t_kv[:, tokens:] = turned(other[:tokens, 2 * D:3 * D])
    ends = [ref[:tokens, 3 * D:].astype(BF16) for ref in (mine, other)]
    sums = product(left_blocks(t_kv, n, blocks), jnp.concatenate(ends, axis=0))
    at = place(send, keep, [[part] for part in four(sums, n)], at)
    y = join(u_gkv, other, pick, o_gkv, y_gkv, 3 * D, 3 * D + KV)
    g_kv[...] = product(u_gkv[...], y) * scale
    small = [g_kv[pl.ds(pl.multiple_of(k * b, 8), k), :] for b in blocks]
    small[0] = small[0] + (BLEND_RATE / 4.0) * st_gkv[...]
    place(send, keep, [[part] for part in small], at)


def identity_rows(rows, extent, start):
    row = lax.broadcasted_iota(jnp.int32, (rows, extent), 0) + start
    column = lax.broadcasted_iota(jnp.int32, (rows, extent), 1)
    return row == column


def scaled_inverse_terms(matrix):
    extent = matrix.shape[0]
    on_diagonal = identity_rows(extent, extent, 0)
    trace = jnp.sum(jnp.where(on_diagonal, matrix, 0.0))
    damped = matrix + jnp.where(on_diagonal, DAMPING * trace / extent, 0.0)
    c = 1.0 / jnp.max(jnp.sum(jnp.abs(damped), axis=1))
    return c, c * damped


def halves(values):
    high = values.astype(BF16)
    return high, (values - high.astype(F32)).astype(BF16)


def times(values, high, low):
    v_high, v_low = halves(values)
    rows = values.shape[0]
    stacked = product(jnp.concatenate([v_high, v_low], axis=0), high)
    return stacked[:rows] + stacked[rows:] + product(v_high, low)


def pieces_of(stacks, q, c):
    near, far = (roles(q, parity) for parity in (c, 1 - c))
    order = [(0, 0, 0), (0, 1, 2), (1, 0, 1), (1, 1, 3)]
    found = []
    for stack, blocks in ((stacks[:2], near), (stacks[2:], far)):
        found += [(stack[which].at[lead], blocks[role]) for which, lead, role in order]
    return found


def assemble(pieces, at, n, width, extent, whole):
    tiles = width // LANES
    for piece, b in pieces:
        parts = [piece[at + n * t:at + n * (t + 1), :] for t in range(tiles)]
        parts += [jnp.zeros((n, LANES), F32)] * (extent // LANES - tiles)
        turned = rolled(jnp.concatenate(parts, axis=1), n * b)
        whole[pl.ds(pl.multiple_of(n * b, 8), n), :] = turned
    windows = whole[...]

    def block_of(axis):
        shape = (extent, 1) if axis == 0 else (1, extent)
        index = lax.broadcasted_iota(jnp.int32, shape, axis)
        return sum([(index >= n * step).astype(jnp.int32) for step in range(1, 8)])

    apart = jnp.bitwise_and(block_of(1) - block_of(0), 7)
    matrix = jnp.where(apart <= 4, windows, windows.T)
    return matrix


def own_rows(ref, q, c, n):
    return ref[pl.ds(pl.multiple_of(n * (2 * q + c), 8), n), :]


def parity_rows(ref, c, n):
    parts = [ref[pl.ds(pl.multiple_of(n * (2 * j + c), 8), n), :] for j in range(4)]
    return jnp.concatenate(parts, axis=0)


def identity_parity(extent, c, n):
    parts = [identity_rows(n, extent, n * (2 * j + c)) for j in range(4)]
    return jnp.concatenate(parts, axis=0)


def left_rows(c, rows, identity, high, low):
    first = jnp.where(identity, 2.0, 0.0) - rows
    second = times(first, high, low)
    third = 2.0 * second - times(second, high, low)
    return c * (2.0 * first - third)


def right_product(values, c, high, low):
    first = 2.0 * values - times(values, high, low)
    second = times(first, high, low)
    third = 2.0 * second - times(second, high, low)
    return c * (2.0 * first - third)


def left_inverse(matrix, c, n, whole, high_ref, low_ref):
    factor, scaled = scaled_inverse_terms(matrix)
    whole[...] = scaled
    high_ref[...], low_ref[...] = halves(scaled)
    return left_rows(
        factor, parity_rows(whole, c, n), identity_parity(whole.shape[0], c, n),
        high_ref[...], low_ref[...],
    )


def left_kernel(n, width, pos, *refs):
    stacks, (new_ref, x_ref, whole, high_ref, low_ref) = refs[:4], refs[4:]
    q, c = pos[0], pos[1]
    matrix = assemble(pieces_of(stacks, q, c), 0, n, width, whole.shape[0], whole)
    whole[...] = matrix
    new_ref[...] = own_rows(whole, q, c, n)
    x_ref[...] = left_inverse(matrix, c, n, whole, high_ref, low_ref)


def middle_kernel(n, pos, x_ref, *refs):
    stacks, (t_ref, rows_ref, s_ref, s_high, s_low) = refs[:4], refs[4:]
    q, c = pos[0], pos[1]
    tiles = s_ref.shape[1] // LANES
    for piece, b in pieces_of(stacks, q, c):
        rows = jnp.concatenate([piece[n * t:n * (t + 1), :] for t in range(tiles)], axis=1)
        at = pl.ds(pl.multiple_of(n * b, 32), n)
        s_ref[at, :] = rows
        s_high[at, :], s_low[at, :] = halves(rows)
    t_ref[...] = times(x_ref[...], s_high[...], s_low[...])
    rows_ref[...] = parity_rows(s_ref, c, n)


def right_kernel(n, width, pos, t_ref, rows_ref, *refs):
    stacks, (new_ref, step_ref, fit_ref, whole, high_ref, low_ref, step_all) = refs[:4], refs[4:]
    q, c = pos[0], pos[1]
    matrix = assemble(pieces_of(stacks, q, c), 0, n, width, whole.shape[0], whole)
    whole[...] = matrix
    new_ref[...] = own_rows(whole, q, c, n)
    factor, scaled = scaled_inverse_terms(matrix)
    high_ref[...], low_ref[...] = halves(scaled)
    step = right_product(t_ref[...], factor, high_ref[...], low_ref[...])
    step_all[...] = step
    step_ref[...] = step_all[pl.ds(pl.multiple_of(n * q, 8), n), :]
    fit_ref[...] = jnp.broadcast_to(jnp.sum(step * rows_ref[...]), fit_ref.shape)


def keyval_kernel(n, k, width, pos, *refs):
    stacks, (new_left, new_right, step_ref, fit_ref) = refs[:4], refs[4:8]
    whole, high_ref, low_ref, grad_ref, g_ref, t_ref = refs[8:]
    q, c = pos[0], pos[1]
    pieces = pieces_of(stacks, q, c)
    at = n * (width // LANES)
    for piece, b in pieces:
        grad_ref[pl.ds(pl.multiple_of(n * b, 8), n), :] = piece[at:at + n, :]
        g_ref[pl.ds(pl.multiple_of(k * b, 8), k), :] = piece[at + n:at + n + k, :]
    matrix = assemble(pieces, 0, n, width, whole.shape[0], whole)
    whole[...] = matrix
    new_left[...] = own_rows(whole, q, c, n)
    new_right[...] = own_rows(g_ref, q, c, k)
    x_rows = left_inverse(matrix, c, n, whole, high_ref, low_ref)
    t_rows = times(x_rows, *halves(grad_ref[...]))
    factor, scaled = scaled_inverse_terms(g_ref[...])
    step = right_product(t_rows, factor, *halves(scaled))
    t_ref[...] = step
    step_ref[...] = t_ref[pl.ds(pl.multiple_of(n * q, 8), n), :]
    fit_ref[...] = jnp.broadcast_to(jnp.sum(step * parity_rows(grad_ref, c, n)), fit_ref.shape)


def update_kernel(fit_own, fit_other, *refs):
    (step_q, step_kv, weight_q, weight_kv, moment_q, moment_kv) = refs[:6]
    outs = refs[6:]
    fitness = (fit_own[...] + fit_other[...])[:1, :1]
    scale = jnp.sqrt(TRUST_BOUND / (LEARNING_RATE * LEARNING_RATE * fitness))
    for step, weight, moment, at in (
        (step_q, weight_q, moment_q, 0), (step_kv, weight_kv, moment_kv, 1)
    ):
        fresh = MOMENTUM * moment[...] + scale * step[...]
        outs[2 + at][...] = fresh
        outs[at][...] = weight[...] - LEARNING_RATE * fresh


def call(kernel, outs, scratch, count, flops=0, scalars=1, kind=F32):
    vmem = pl.BlockSpec(memory_space=pltpu.VMEM)
    smem = pl.BlockSpec(memory_space=pltpu.SMEM)
    return pl.pallas_call(
        kernel,
        out_shape=[jax.ShapeDtypeStruct(shape, kind) for shape in outs],
        in_specs=[smem] * scalars + [vmem] * (count - scalars),
        out_specs=[vmem] * len(outs),
        scratch_shapes=[pltpu.VMEM(shape, kind) for shape, kind in scratch],
        compiler_params=pltpu.CompilerParams(vmem_limit_bytes=VMEM_LIMIT),
        cost_estimate=pl.CostEstimate(flops=flops, bytes_accessed=4_000_000, transcendentals=0),
    )


def core_flip(value):
    return lax.ppermute(value, "dp", [(i, i ^ 1) for i in range(8)])


def first_hop(value):
    return lax.ppermute(value, "dp", [(i, i ^ (4 if i & 1 else 2)) for i in range(8)])


def second_hop(value):
    return lax.ppermute(value, "dp", [(i, i ^ (2 if i & 1 else 4)) for i in range(8)])


def plane_flip(value, bit):
    return lax.ppermute(value, "group", [(i, i ^ bit) for i in range(4)])


def after(value, *others):
    return lax.optimization_barrier((value,) + others)[0]


def plane_halves(piece):
    half = piece.shape[0] // 2
    even = lax.axis_index("group") % 2 == 0
    low, high = piece[:half], piece[half:]
    return jnp.where(even, low, high), jnp.where(even, high, low)


def plane_whole(mine, theirs):
    even = lax.axis_index("group") % 2 == 0
    return jnp.concatenate(
        [jnp.where(even, mine, theirs), jnp.where(even, theirs, mine)], axis=0
    )


ORDER = (
    "+Ars1", "+Krs1", "+Srs1", "-Ars1", "+Ars2", "-Krs1", "+Krs2", "-Ars2", "+Az1", "-Srs1",
    "+Srs2", "+Grs1", "-Krs2", "+Kz1", "-Az1", "+Az2", "-Srs2", "+Sz1", "-Kz1", "+Kz2", "-Grs1",
    "+Grs2", "-Az2", "+Az3", "-Sz1", "+Sz2", "-Grs2", "+Gz1", "-Az3", "+Aag1", "-Kz2", "+Kz3",
    "-Gz1", "+Gz2", "-Aag1", "+Acn", "+Aag2", "-Sz2", "+Sz3", "-Kz3", "-Acn", "+Kag1", "-Gz2",
    "+Gz3", "-Sz3", "+Sag1", "-Aag2", "+Acf", "-Kag1", "+Kcn", "+Kag2", "-Gz3", "-Acf", "+Gag1",
    "-Kcn", "kA", "-Sag1", "-Gag1", "+Scn", "+Sag2", "-Kag2", "+Kcf", "-Scn", "+Gcn", "+Gag2",
    "-Kcf", "kK", "-Gcn", "-Sag2", "+Scf", "-Gag2", "+Gcf", "-Scf", "kT", "-Gcf", "kG",
)


class Transfers:
    def __init__(self, sends, keeps):
        self.got = {}
        self.flying = {}
        self.sends, self.keeps = sends, keeps
        self.token = None

    def operand(self, chunk, step):
        got = self.got
        if step == "rs1":
            return self.sends[chunk]
        if step == "rs2":
            return self.keeps[chunk][1] + got[chunk, "rs1"][1]
        if step == "z1":
            own = self.keeps[chunk][0] + got[chunk, "rs1"][0] + got[chunk, "rs2"]
            got[chunk, "half"], theirs = plane_halves(own)
            return theirs
        if step == "z2":
            got[chunk, "half"] = got[chunk, "half"] + got[chunk, "z1"]
            return got[chunk, "half"]
        if step == "z3":
            got[chunk, "half"] = got[chunk, "half"] + got[chunk, "z2"]
            return got[chunk, "half"]
        if step == "ag1":
            got[chunk, "own"] = plane_whole(got[chunk, "half"], got[chunk, "z3"])
            return got[chunk, "own"]
        if step == "ag2":
            got[chunk, "near"] = jnp.stack([got[chunk, "own"], got[chunk, "ag1"]])
            return got[chunk, "near"]
        if step == "cn":
            if (chunk, "near") not in got:
                got[chunk, "near"] = jnp.stack([got[chunk, "own"], got[chunk, "ag1"]])
            return got[chunk, "near"]
        return got[chunk, "ag2"]

    hops = {
        "rs1": first_hop, "rs2": second_hop, "ag1": second_hop, "ag2": first_hop,
        "z1": lambda value: plane_flip(value, 1), "z2": lambda value: plane_flip(value, 2),
        "z3": lambda value: plane_flip(value, 1), "cn": core_flip, "cf": core_flip,
    }

    def start(self, chunk, step):
        value = self.operand(chunk, step)
        if self.token is not None:
            value = after(value, self.token)
        self.flying[chunk, step] = self.hops[step](value)

    def passed(self, value):
        if self.token is not None:
            value, _ = lax.optimization_barrier((value, self.token))
        self.token = value
        return value

    def wait(self, chunk, step):
        self.got[chunk, step] = self.passed(self.flying.pop((chunk, step)))

    def stacks(self, chunk):
        return [self.got[chunk, step] for step in ("near", "ag2", "cn", "cf")]


def fast_shards(
    act_query, grad_query, act_keyval, grad_keyval, sample_rows,
    state_aq, state_gq, state_akv, state_gkv,
    weight_query, weight_keyval, moment_query, moment_keyval,
):
    D, KV = act_query.shape[1], grad_keyval.shape[1]
    n, k = state_aq.shape[0], state_gkv.shape[0]
    tokens, samples = act_query.shape[0], sample_rows.shape[0]
    width = -(-5 * n // LANES) * LANES
    d = lax.axis_index("dp")
    pos = jnp.stack([d // 2, d % 2]).astype(jnp.int32)
    scale = (1.0 - BLEND_RATE) / (samples * 32)

    (mine,) = call(cast_kernel, [(tokens + 8, 3 * D + KV)], [], 5, scalars=0)(
        sample_rows.reshape(1, samples), act_query, grad_query, act_keyval, grad_keyval
    )
    other = core_flip(mine)
    y_aq, y_gq, y_akv, y_gkv, u_aq, u_gq, u_akv, u_gkv, t_q, t_kv = call(
        functools.partial(own_kernel, tokens, samples, D),
        [(samples, D)] * 3 + [(samples, KV)] + [(D, samples)] * 3 + [(KV, samples)]
        + [(D, tokens)] * 2,
        [], 1, 300_000_000, scalars=0, kind=BF16,
    )(mine)

    r_f = n * (width // LANES)
    both, all_tokens = ((D, 2 * samples), BF16), ((D, 2 * tokens), BF16)
    sends, keeps = {}, {}
    sends["A"], keeps["A"] = call(
        functools.partial(factor_kernel, n, width, scale, 0), [(2, r_f, LANES)] * 2,
        [both], 5, 300_000_000,
    )(pos, other, y_aq, u_aq, state_aq)
    sends["K"], keeps["K"] = call(
        functools.partial(keyval_sums_kernel, n, k, width, scale),
        [(2, r_f + n + k, LANES)] * 2,
        [both, ((KV, 2 * samples), BF16), all_tokens, ((KV, KV), F32)], 10, 400_000_000,
    )(pos, mine, other, y_akv, y_gkv, u_akv, u_gkv, t_kv, state_akv, state_gkv)
    sends["S"], keeps["S"] = call(
        functools.partial(gradient_kernel, n), [(2, n * (D // LANES), LANES)] * 2,
        [all_tokens], 4, 500_000_000,
    )(pos, mine, other, t_q)
    sends["G"], keeps["G"] = call(
        functools.partial(factor_kernel, n, width, scale, D), [(2, r_f, LANES)] * 2,
        [both], 5, 300_000_000,
    )(pos, other, y_gq, u_gq, state_gq)

    rows = (4 * n, D)
    square = [((D, D), F32), ((D, D), BF16), ((D, D), BF16)]
    fit = (8, LANES)
    moves = Transfers(sends, keeps)
    for item in ORDER:
        if item[0] == "+":
            moves.start(item[1], item[2:])
        elif item[0] == "-":
            moves.wait(item[1], item[2:])
        elif item == "kA":
            new_aq, x_rows = call(
                functools.partial(left_kernel, n, width), [(n, D), rows], square, 5, 2_000_000_000
            )(after(pos, moves.token), *moves.stacks("A"))
            x_rows = moves.passed(x_rows)
        elif item == "kK":
            new_akv, new_gkv, step_kv, fit_kv = call(
                functools.partial(keyval_kernel, n, k, width),
                [(n, D), (k, KV), (n, KV), fit],
                square + [((D, KV), F32), ((KV, KV), F32), ((4 * n, KV), F32)],
                5, 3_000_000_000,
            )(after(pos, moves.token), *moves.stacks("K"))
            fit_kv = moves.passed(fit_kv)
        elif item == "kT":
            t_rows, s_rows = call(
                functools.partial(middle_kernel, n), [rows, rows], square, 6, 1_000_000_000
            )(after(pos, moves.token), x_rows, *moves.stacks("S"))
            t_rows = moves.passed(t_rows)
        else:
            new_gq, step_q, fit_q = call(
                functools.partial(right_kernel, n, width), [(n, D), (n, D), fit],
                square + [(rows, F32)], 7, 3_000_000_000,
            )(pos, t_rows, s_rows, *moves.stacks("G"))

    part = fit_q + fit_kv
    weight_q, weight_kv, moment_q, moment_kv = call(
        update_kernel, [(n, D), (n, KV)] * 2, [], 8, scalars=0
    )(
        part, core_flip(part), step_q, step_kv,
        weight_query, weight_keyval, moment_query, moment_keyval,
    )
    return (new_aq, new_gq, new_akv, new_gkv, weight_q, weight_kv, moment_q, moment_kv)


def from_root(value, axis, source):
    kept = jnp.where(lax.axis_index(axis) == source, value, 0).astype(value.dtype)
    return lax.psum(kept, axis)


def newton(damped):
    extent = damped.shape[0]
    identity = jnp.eye(extent, dtype=jnp.float32)
    inverse_norm = 1.0 / jnp.max(jnp.sum(jnp.abs(damped), axis=1))
    iterate = inverse_norm * (2.0 * identity - inverse_norm * damped)
    product = jnp.dot(damped, iterate, precision=PRECISE)
    iterate = jnp.dot(iterate, 2.0 * identity - product, precision=PRECISE)
    return iterate


def damped_inverse(factor):
    extent = factor.shape[0]
    identity = jnp.eye(extent, dtype=jnp.float32)
    return newton(factor + DAMPING * jnp.trace(factor) / extent * identity)


def precondition(left_inverse, gradient, right_inverse):
    return jnp.dot(
        jnp.dot(left_inverse, gradient, precision=PRECISE), right_inverse, precision=PRECISE
    )


def inner_rows(first_block, second_block):
    return lax.dot_general(
        first_block, second_block, (((0,), (0,)), ((), ())), preferred_element_type=jnp.float32
    )


def deliver(matrix, holder):
    return from_root(matrix, ("dp", "group"), holder)


def owner_step(left_factor, right_factor, gradient):
    return precondition(damped_inverse(left_factor), gradient, damped_inverse(right_factor))


def shards(
    act_query,
    grad_query,
    act_keyval,
    grad_keyval,
    sample_rows,
    state_aq,
    state_gq,
    state_akv,
    state_gkv,
    weight_query,
    weight_keyval,
    moment_query,
    moment_keyval,
):
    devices = lax.axis_size("dp") * lax.axis_size("group")
    total_samples = sample_rows.shape[0] * devices
    flat_index = lax.axis_index("dp") * lax.axis_size("group") + lax.axis_index("group")
    extent = state_aq.shape[0]
    start = lax.axis_index("dp") * extent

    def covariance(tokens_block):
        chosen = jnp.take(tokens_block, sample_rows, axis=0)
        return inner_rows(chosen, chosen)

    local_terms = (
        covariance(act_query),
        covariance(grad_query),
        covariance(act_keyval),
        covariance(grad_keyval),
        inner_rows(act_query, grad_query),
        inner_rows(act_keyval, grad_keyval),
    )
    shares = (
        lax.psum_scatter(local_terms[0], "dp", scatter_dimension=0, tiled=True),
        lax.psum_scatter(local_terms[1], "dp", scatter_dimension=0, tiled=True),
        lax.psum_scatter(local_terms[2], "dp", scatter_dimension=0, tiled=True),
        lax.psum_scatter(local_terms[3], "dp", scatter_dimension=0, tiled=True),
        lax.psum_scatter(local_terms[4], "dp", scatter_dimension=0, tiled=True),
        lax.psum_scatter(local_terms[5], "dp", scatter_dimension=0, tiled=True),
    )
    totals = lax.psum((shares[0], shares[1], shares[2], shares[3], shares[4], shares[5]), "group")
    cov_aq, cov_gq, cov_akv, cov_gkv, rows_q, rows_kv = totals
    new_aq = BLEND_RATE * state_aq + (1.0 - BLEND_RATE) * (cov_aq / total_samples)
    new_gq = BLEND_RATE * state_gq + (1.0 - BLEND_RATE) * (cov_gq / total_samples)
    new_akv = BLEND_RATE * state_akv + (1.0 - BLEND_RATE) * (cov_akv / total_samples)
    new_gkv = BLEND_RATE * state_gkv + (1.0 - BLEND_RATE) * (cov_gkv / total_samples)
    gathered = (
        lax.all_gather(new_aq, "dp", axis=0, tiled=True),
        lax.all_gather(new_gq, "dp", axis=0, tiled=True),
        lax.all_gather(new_akv, "dp", axis=0, tiled=True),
        lax.all_gather(new_gkv, "dp", axis=0, tiled=True),
        lax.all_gather(rows_q, "dp", axis=0, tiled=True),
        lax.all_gather(rows_kv, "dp", axis=0, tiled=True),
    )
    whole_aq, whole_gq, whole_akv, whole_gkv, whole_sum_q, whole_sum_kv = gathered
    holders = (0, 0, 1, 1)
    pairs = (
        (whole_aq, whole_gq, whole_sum_q, rows_q, holders[0], holders[1]),
        (whole_akv, whole_gkv, whole_sum_kv, rows_kv, holders[2], holders[3]),
    )
    step_rows = []
    fitness = jnp.zeros((), jnp.float32)
    for left_factor, right_factor, gradient, gradient_rows, left_holder, right_holder in pairs:
        whole_step = lax.cond(
            flat_index == left_holder,
            owner_step,
            lambda first, second, third: jnp.zeros_like(third),
            left_factor,
            right_factor,
            gradient,
        )
        whole_step = deliver(whole_step, left_holder)
        fitness = fitness + jnp.sum(whole_step * gradient)
        step_rows.append(lax.dynamic_slice_in_dim(whole_step, start, extent, 0))
    scale = jnp.sqrt(TRUST_BOUND / (LEARNING_RATE * LEARNING_RATE * fitness))
    moment_q = MOMENTUM * moment_query + scale * step_rows[0]
    moment_kv = MOMENTUM * moment_keyval + scale * step_rows[1]
    weight_q = weight_query - LEARNING_RATE * moment_q
    weight_kv = weight_keyval - LEARNING_RATE * moment_kv
    return (new_aq, new_gq, new_akv, new_gkv, weight_q, weight_kv, moment_q, moment_kv)


def solution(mesh):
    placed = (
        P(("dp", "group"), None),
        P(("dp", "group"), None),
        P(("dp", "group"), None),
        P(("dp", "group"), None),
        P(("dp", "group")),
        P("dp", None),
        P("dp", None),
        P("dp", None),
        P("dp", None),
        P("dp", None),
        P("dp", None),
        P("dp", None),
        P("dp", None),
    )
    plane = mesh.shape["dp"] == 8 and mesh.shape["group"] == 4
    return jax.shard_map(
        fast_shards if plane else shards,
        mesh=mesh,
        in_specs=placed,
        out_specs=(
            P("dp", None),
            P("dp", None),
            P("dp", None),
            P("dp", None),
            P("dp", None),
            P("dp", None),
            P("dp", None),
            P("dp", None),
        ),
        check_vma=False,
    )
```

```python
import functools

import jax
import jax.numpy as jnp
from jax import lax
from jax.experimental import pallas as pl
from jax.experimental.pallas import tpu as pltpu
from jax.sharding import PartitionSpec as P

PRECISE = lax.Precision.HIGHEST
BLEND_RATE = 0.8
DAMPING = 0.05
MOMENTUM = 0.9
LEARNING_RATE = 0.001
TRUST_BOUND = 0.5
LANES = 128
F32 = jnp.float32
BF16 = jnp.bfloat16


def rolled(block, shift):
    return pltpu.roll(block, shift, 1)


def window_tiles(block, start, width):
    extent = block.shape[1]
    shift = lax.rem(extent - start, extent)
    turned = rolled(block, shift)
    return [turned[:, LANES * t:LANES * (t + 1)] for t in range(width // LANES)]


def plain_tiles(block):
    return [block[:, LANES * t:LANES * (t + 1)] for t in range(block.shape[1] // LANES)]


def write_tiles(ref, lead, tiles, at=0):
    for tile in tiles:
        ref[lead, at:at + tile.shape[0], :] = tile
        at += tile.shape[0]
    return at


def product(first, second):
    return lax.dot_general(
        first, second, (((1,), (0,)), ((), ())), preferred_element_type=F32
    )


def cast_kernel(rows, aq, gq, akv, gkv, out):
    at, tokens = 0, aq.shape[0]
    for ref in (aq, gq, akv, gkv):
        out[:tokens, at:at + ref.shape[1]] = ref[...].astype(F32)
        at += ref.shape[1]
    out[tokens:, :] = jnp.zeros((out.shape[0] - tokens, at), F32)
    out[tokens:tokens + 1, :rows.shape[1]] = rows[...].astype(F32)


def picker(all_tokens, tokens, samples):
    rows = all_tokens[tokens:tokens + 1, :samples].astype(jnp.int32)
    token = lax.broadcasted_iota(jnp.int32, (tokens, samples), 0)
    return (token == rows).astype(F32).T.astype(BF16)


def turned(values):
    return values.astype(F32).T.astype(BF16)


def own_kernel(tokens, samples, D, mine, y_aq, y_gq, y_akv, y_gkv, u_aq, u_gq, u_akv, u_gkv, t_q, t_kv):
    pick = picker(mine, tokens, samples)
    at = 0
    for y, u in ((y_aq, u_aq), (y_gq, u_gq), (y_akv, u_akv), (y_gkv, u_gkv)):
        chosen = product(pick, mine[:tokens, at:at + y.shape[1]].astype(BF16))
        y[...] = chosen.astype(BF16)
        u[...] = chosen.T.astype(BF16)
        at += y.shape[1]
    t_q[...] = turned(mine[:tokens, :D])
    t_kv[...] = turned(mine[:tokens, 2 * D:3 * D])


def roles(q, c):
    return [2 * chip + c for chip in (q, q ^ (1 + c), q ^ (2 - c), q ^ 3)]


def join(u, other, pick, own_u, own_y, lo, hi):
    samples, tokens = pick.shape
    chosen = product(pick, other[:tokens, lo:hi].astype(BF16))
    u[:, :samples] = own_u[...]
    u[:, samples:] = chosen.T.astype(BF16)
    return jnp.concatenate([own_y[...], chosen.astype(BF16)], axis=0)


def left_blocks(ref, n, blocks):
    parts = [ref[pl.ds(pl.multiple_of(n * b, 32), n), :] for b in blocks]
    return jnp.concatenate(parts, axis=0)


def four(values, n):
    return [values[n * r:n * (r + 1)] for r in range(4)]


def place(send, keep, tiles, at=0):
    write_tiles(send, 0, tiles[1], at)
    write_tiles(send, 1, tiles[3], at)
    write_tiles(keep, 0, tiles[0], at)
    return write_tiles(keep, 1, tiles[2], at)


def factor_tiles(u, y, state, n, blocks, width, scale):
    parts = four(product(left_blocks(u, n, blocks), y) * scale, n)
    parts[0] = parts[0] + (BLEND_RATE / 4.0) * state[...]
    return [window_tiles(part, n * b, width) for part, b in zip(parts, blocks)]


def gram_kernel(
    n, k, width, scale,
    pos, mine, other, y_aq, y_gq, y_akv, y_gkv, o_aq, o_gq, o_akv, o_gkv, o_q, o_kv,
    st_aq, st_gq, st_akv, st_gkv,
    a_send, a_keep, k_send, k_keep, s_send, s_keep, g_send, g_keep,
    u_aq, u_gq, u_akv, u_gkv, t_q, t_kv, g_kv,
):
    tokens, samples = o_kv.shape[1], o_akv.shape[1]
    D, KV = y_akv.shape[1], y_gkv.shape[1]
    blocks = roles(pos[0], pos[1])
    pick = picker(other, tokens, samples)

    def factor(u, o, y, state, lo):
        chosen = join(u, other, pick, o, y, lo, lo + D)
        return factor_tiles(u, chosen, state, n, blocks, width, scale)

    def gradient(t, o, lo, first, last):
        t[:, :tokens] = o[...]
        t[:, tokens:] = turned(other[:tokens, lo:lo + D])
        ends = [ref[:tokens, first:last].astype(BF16) for ref in (mine, other)]
        return four(product(left_blocks(t, n, blocks), jnp.concatenate(ends, axis=0)), n)

    place(a_send, a_keep, factor(u_aq, o_aq, y_aq, st_aq, 0))
    at = place(k_send, k_keep, factor(u_akv, o_akv, y_akv, st_akv, 2 * D))
    sums = gradient(t_kv, o_kv, 2 * D, 3 * D, 3 * D + KV)
    at = place(k_send, k_keep, [[part] for part in sums], at)
    chosen = join(u_gkv, other, pick, o_gkv, y_gkv, 3 * D, 3 * D + KV)
    g_kv[...] = product(u_gkv[...], chosen) * scale
    small = [g_kv[pl.ds(pl.multiple_of(k * b, 8), k), :] for b in blocks]
    small[0] = small[0] + (BLEND_RATE / 4.0) * st_gkv[...]
    place(k_send, k_keep, [[part] for part in small], at)
    place(s_send, s_keep, [plain_tiles(part) for part in gradient(t_q, o_q, 0, D, 2 * D)])
    place(g_send, g_keep, factor(u_gq, o_gq, y_gq, st_gq, D))


def identity_rows(rows, extent, start):
    row = lax.broadcasted_iota(jnp.int32, (rows, extent), 0) + start
    column = lax.broadcasted_iota(jnp.int32, (rows, extent), 1)
    return row == column


def scaled_inverse_terms(matrix):
    extent = matrix.shape[0]
    on_diagonal = identity_rows(extent, extent, 0)
    trace = jnp.sum(jnp.where(on_diagonal, matrix, 0.0))
    damped = matrix + jnp.where(on_diagonal, DAMPING * trace / extent, 0.0)
    c = 1.0 / jnp.max(jnp.sum(jnp.abs(damped), axis=1))
    return c, c * damped


def halves(values):
    high = values.astype(BF16)
    return high, (values - high.astype(F32)).astype(BF16)


def times(values, high, low):
    v_high, v_low = halves(values)
    rows = values.shape[0]
    stacked = product(jnp.concatenate([v_high, v_low], axis=0), high)
    return stacked[:rows] + stacked[rows:] + product(v_high, low)


def pieces_of(stacks, q, c):
    near, far = (roles(q, parity) for parity in (c, 1 - c))
    order = [(0, 0, 0), (0, 1, 2), (1, 0, 1), (1, 1, 3)]
    found = []
    for stack, blocks in ((stacks[:2], near), (stacks[2:], far)):
        found += [(stack[which].at[lead], blocks[role]) for which, lead, role in order]
    return found


def assemble(pieces, at, n, width, extent, whole):
    tiles = width // LANES
    for piece, b in pieces:
        parts = [piece[at + n * t:at + n * (t + 1), :] for t in range(tiles)]
        parts += [jnp.zeros((n, LANES), F32)] * (extent // LANES - tiles)
        turned = rolled(jnp.concatenate(parts, axis=1), n * b)
        whole[pl.ds(pl.multiple_of(n * b, 8), n), :] = turned
    windows = whole[...]

    def block_of(axis):
        shape = (extent, 1) if axis == 0 else (1, extent)
        index = lax.broadcasted_iota(jnp.int32, shape, axis)
        return sum([(index >= n * step).astype(jnp.int32) for step in range(1, 8)])

    apart = jnp.bitwise_and(block_of(1) - block_of(0), 7)
    matrix = jnp.where(apart <= 4, windows, windows.T)
    return matrix


def own_rows(ref, q, c, n):
    return ref[pl.ds(pl.multiple_of(n * (2 * q + c), 8), n), :]


def parity_rows(ref, c, n):
    parts = [ref[pl.ds(pl.multiple_of(n * (2 * j + c), 8), n), :] for j in range(4)]
    return jnp.concatenate(parts, axis=0)


def identity_parity(extent, c, n):
    parts = [identity_rows(n, extent, n * (2 * j + c)) for j in range(4)]
    return jnp.concatenate(parts, axis=0)


def left_rows(c, rows, identity, high, low):
    first = jnp.where(identity, 2.0, 0.0) - rows
    second = times(first, high, low)
    third = 2.0 * second - times(second, high, low)
    return c * (2.0 * first - third)


def right_product(values, c, high, low):
    first = 2.0 * values - times(values, high, low)
    second = times(first, high, low)
    third = 2.0 * second - times(second, high, low)
    return c * (2.0 * first - third)


def left_inverse(matrix, c, n, whole, high_ref, low_ref):
    factor, scaled = scaled_inverse_terms(matrix)
    whole[...] = scaled
    high_ref[...], low_ref[...] = halves(scaled)
    return left_rows(
        factor, parity_rows(whole, c, n), identity_parity(whole.shape[0], c, n),
        high_ref[...], low_ref[...],
    )


def left_kernel(n, width, pos, *refs):
    stacks, (new_ref, x_ref, whole, high_ref, low_ref) = refs[:4], refs[4:]
    q, c = pos[0], pos[1]
    matrix = assemble(pieces_of(stacks, q, c), 0, n, width, whole.shape[0], whole)
    whole[...] = matrix
    new_ref[...] = own_rows(whole, q, c, n)
    x_ref[...] = left_inverse(matrix, c, n, whole, high_ref, low_ref)


def middle_kernel(n, pos, x_ref, *refs):
    stacks, (t_ref, rows_ref, s_ref, s_high, s_low) = refs[:4], refs[4:]
    q, c = pos[0], pos[1]
    tiles = s_ref.shape[1] // LANES
    for piece, b in pieces_of(stacks, q, c):
        rows = jnp.concatenate([piece[n * t:n * (t + 1), :] for t in range(tiles)], axis=1)
        at = pl.ds(pl.multiple_of(n * b, 32), n)
        s_ref[at, :] = rows
        s_high[at, :], s_low[at, :] = halves(rows)
    t_ref[...] = times(x_ref[...], s_high[...], s_low[...])
    rows_ref[...] = parity_rows(s_ref, c, n)


def right_kernel(n, width, pos, t_ref, rows_ref, *refs):
    stacks, (new_ref, step_ref, fit_ref, whole, high_ref, low_ref, step_all) = refs[:4], refs[4:]
    q, c = pos[0], pos[1]
    matrix = assemble(pieces_of(stacks, q, c), 0, n, width, whole.shape[0], whole)
    whole[...] = matrix
    new_ref[...] = own_rows(whole, q, c, n)
    factor, scaled = scaled_inverse_terms(matrix)
    high_ref[...], low_ref[...] = halves(scaled)
    step = right_product(t_ref[...], factor, high_ref[...], low_ref[...])
    step_all[...] = step
    step_ref[...] = step_all[pl.ds(pl.multiple_of(n * q, 8), n), :]
    fit_ref[...] = jnp.broadcast_to(jnp.sum(step * rows_ref[...]), fit_ref.shape)


def keyval_kernel(n, k, width, pos, *refs):
    stacks, (new_left, new_right, step_ref, fit_ref) = refs[:4], refs[4:8]
    whole, high_ref, low_ref, grad_ref, g_ref, t_ref = refs[8:]
    q, c = pos[0], pos[1]
    pieces = pieces_of(stacks, q, c)
    at = n * (width // LANES)
    for piece, b in pieces:
        grad_ref[pl.ds(pl.multiple_of(n * b, 8), n), :] = piece[at:at + n, :]
        g_ref[pl.ds(pl.multiple_of(k * b, 8), k), :] = piece[at + n:at + n + k, :]
    matrix = assemble(pieces, 0, n, width, whole.shape[0], whole)
    whole[...] = matrix
    new_left[...] = own_rows(whole, q, c, n)
    new_right[...] = own_rows(g_ref, q, c, k)
    x_rows = left_inverse(matrix, c, n, whole, high_ref, low_ref)
    t_rows = times(x_rows, *halves(grad_ref[...]))
    factor, scaled = scaled_inverse_terms(g_ref[...])
    step = right_product(t_rows, factor, *halves(scaled))
    t_ref[...] = step
    step_ref[...] = t_ref[pl.ds(pl.multiple_of(n * q, 8), n), :]
    fit_ref[...] = jnp.broadcast_to(jnp.sum(step * parity_rows(grad_ref, c, n)), fit_ref.shape)


def update_kernel(fit_own, fit_other, *refs):
    (step_q, step_kv, weight_q, weight_kv, moment_q, moment_kv) = refs[:6]
    outs = refs[6:]
    fitness = (fit_own[...] + fit_other[...])[:1, :1]
    scale = jnp.sqrt(TRUST_BOUND / (LEARNING_RATE * LEARNING_RATE * fitness))
    for step, weight, moment, at in (
        (step_q, weight_q, moment_q, 0), (step_kv, weight_kv, moment_kv, 1)
    ):
        fresh = MOMENTUM * moment[...] + scale * step[...]
        outs[2 + at][...] = fresh
        outs[at][...] = weight[...] - LEARNING_RATE * fresh


def call(kernel, outs, scratch, count, flops=0, scalars=1, kind=F32, limit=24):
    vmem = pl.BlockSpec(memory_space=pltpu.VMEM)
    smem = pl.BlockSpec(memory_space=pltpu.SMEM)
    return pl.pallas_call(
        kernel,
        out_shape=[jax.ShapeDtypeStruct(shape, kind) for shape in outs],
        in_specs=[smem] * scalars + [vmem] * (count - scalars),
        out_specs=[vmem] * len(outs),
        scratch_shapes=[pltpu.VMEM(shape, kind) for shape, kind in scratch],
        compiler_params=pltpu.CompilerParams(vmem_limit_bytes=limit * 1024 * 1024),
        cost_estimate=pl.CostEstimate(flops=flops, bytes_accessed=4_000_000, transcendentals=0),
    )


def core_flip(value):
    return lax.ppermute(value, "dp", [(i, i ^ 1) for i in range(8)])


def first_hop(value):
    return lax.ppermute(value, "dp", [(i, i ^ (4 if i & 1 else 2)) for i in range(8)])


def second_hop(value):
    return lax.ppermute(value, "dp", [(i, i ^ (2 if i & 1 else 4)) for i in range(8)])


def plane_flip(value, bit):
    return lax.ppermute(value, "group", [(i, i ^ bit) for i in range(4)])


def after(value, *others):
    return lax.optimization_barrier((value,) + others)[0]


def plane_halves(piece):
    half = piece.shape[0] // 2
    even = lax.axis_index("group") % 2 == 0
    low, high = piece[:half], piece[half:]
    return jnp.where(even, low, high), jnp.where(even, high, low)


def plane_whole(mine, theirs):
    even = lax.axis_index("group") % 2 == 0
    return jnp.concatenate(
        [jnp.where(even, mine, theirs), jnp.where(even, theirs, mine)], axis=0
    )


ORDER = (
    "+Ars1", "+Krs1", "+Srs1", "-Ars1", "+Ars2", "-Krs1", "+Krs2", "-Ars2", "+Az1", "-Srs1",
    "+Srs2", "+Grs1", "-Krs2", "+Kz1", "-Az1", "+Az2", "-Srs2", "+Sz1", "-Kz1", "+Kz2", "-Grs1",
    "+Grs2", "-Az2", "+Az3", "-Sz1", "+Sz2", "-Grs2", "+Gz1", "-Az3", "+Aag1", "-Kz2", "+Kz3",
    "-Gz1", "+Gz2", "-Aag1", "+Acn", "+Aag2", "-Sz2", "+Sz3", "-Kz3", "-Acn", "+Kag1", "-Gz2",
    "+Gz3", "-Sz3", "+Sag1", "-Aag2", "+Acf", "-Kag1", "+Kcn", "+Kag2", "-Gz3", "-Acf", "+Gag1",
    "-Kcn", "kA", "-Sag1", "-Gag1", "+Scn", "+Sag2", "-Kag2", "+Kcf", "-Scn", "+Gcn", "+Gag2",
    "-Kcf", "kK", "-Gcn", "-Sag2", "+Scf", "-Gag2", "+Gcf", "-Scf", "kT", "-Gcf", "kG",
)


class Transfers:
    def __init__(self, sends, keeps):
        self.got = {}
        self.flying = {}
        self.sends, self.keeps = sends, keeps
        self.token = None

    def operand(self, chunk, step):
        got = self.got
        if step == "rs1":
            return self.sends[chunk]
        if step == "rs2":
            return self.keeps[chunk][1] + got[chunk, "rs1"][1]
        if step == "z1":
            own = self.keeps[chunk][0] + got[chunk, "rs1"][0] + got[chunk, "rs2"]
            got[chunk, "half"], theirs = plane_halves(own)
            return theirs
        if step == "z2":
            got[chunk, "half"] = got[chunk, "half"] + got[chunk, "z1"]
            return got[chunk, "half"]
        if step == "z3":
            got[chunk, "half"] = got[chunk, "half"] + got[chunk, "z2"]
            return got[chunk, "half"]
        if step == "ag1":
            got[chunk, "own"] = plane_whole(got[chunk, "half"], got[chunk, "z3"])
            return got[chunk, "own"]
        if step == "ag2":
            got[chunk, "near"] = jnp.stack([got[chunk, "own"], got[chunk, "ag1"]])
            return got[chunk, "near"]
        if step == "cn":
            if (chunk, "near") not in got:
                got[chunk, "near"] = jnp.stack([got[chunk, "own"], got[chunk, "ag1"]])
            return got[chunk, "near"]
        return got[chunk, "ag2"]

    hops = {
        "rs1": first_hop, "rs2": second_hop, "ag1": second_hop, "ag2": first_hop,
        "z1": lambda value: plane_flip(value, 1), "z2": lambda value: plane_flip(value, 2),
        "z3": lambda value: plane_flip(value, 1), "cn": core_flip, "cf": core_flip,
    }

    def start(self, chunk, step):
        value = self.operand(chunk, step)
        if self.token is not None:
            value = after(value, self.token)
        self.flying[chunk, step] = self.hops[step](value)

    def passed(self, value):
        if self.token is not None:
            value, _ = lax.optimization_barrier((value, self.token))
        self.token = value
        return value

    def wait(self, chunk, step):
        self.got[chunk, step] = self.passed(self.flying.pop((chunk, step)))

    def stacks(self, chunk):
        return [self.got[chunk, step] for step in ("near", "ag2", "cn", "cf")]


def fast_shards(
    act_query, grad_query, act_keyval, grad_keyval, sample_rows,
    state_aq, state_gq, state_akv, state_gkv,
    weight_query, weight_keyval, moment_query, moment_keyval,
):
    D, KV = act_query.shape[1], grad_keyval.shape[1]
    n, k = state_aq.shape[0], state_gkv.shape[0]
    tokens, samples = act_query.shape[0], sample_rows.shape[0]
    width = -(-5 * n // LANES) * LANES
    d = lax.axis_index("dp")
    pos = jnp.stack([d // 2, d % 2]).astype(jnp.int32)
    scale = (1.0 - BLEND_RATE) / (samples * 32)

    (mine,) = call(cast_kernel, [(tokens + 8, 3 * D + KV)], [], 5, scalars=0, limit=8)(
        sample_rows.reshape(1, samples), act_query, grad_query, act_keyval, grad_keyval
    )
    other = core_flip(mine)
    y_aq, y_gq, y_akv, y_gkv, u_aq, u_gq, u_akv, u_gkv, t_q, t_kv = call(
        functools.partial(own_kernel, tokens, samples, D),
        [(samples, D)] * 3 + [(samples, KV)] + [(D, samples)] * 3 + [(KV, samples)]
        + [(D, tokens)] * 2,
        [], 1, 300_000_000, scalars=0, kind=BF16, limit=12,
    )(mine)

    r_f = n * (width // LANES)
    sizes = (r_f, r_f + n + k, n * (D // LANES), r_f)
    grams = call(
        functools.partial(gram_kernel, n, k, width, scale),
        [(2, size, LANES) for size in sizes for _ in range(2)],
        [
            *[((D, 2 * samples), BF16)] * 3, ((KV, 2 * samples), BF16),
            *[((D, 2 * tokens), BF16)] * 2, ((KV, KV), F32),
        ],
        17, 2_000_000_000, limit=16,
    )(
        pos, mine, other, y_aq, y_gq, y_akv, y_gkv, u_aq, u_gq, u_akv, u_gkv, t_q, t_kv,
        state_aq, state_gq, state_akv, state_gkv,
    )
    sends, keeps = dict(zip("AKSG", grams[0::2])), dict(zip("AKSG", grams[1::2]))

    rows = (4 * n, D)
    square = [((D, D), F32), ((D, D), BF16), ((D, D), BF16)]
    fit = (8, LANES)
    moves = Transfers(sends, keeps)
    for item in ORDER:
        if item[0] == "+":
            moves.start(item[1], item[2:])
        elif item[0] == "-":
            moves.wait(item[1], item[2:])
        elif item == "kA":
            new_aq, x_rows = call(
                functools.partial(left_kernel, n, width), [(n, D), rows], square, 5, 2_000_000_000
            )(after(pos, moves.token), *moves.stacks("A"))
            x_rows = moves.passed(x_rows)
        elif item == "kK":
            new_akv, new_gkv, step_kv, fit_kv = call(
                functools.partial(keyval_kernel, n, k, width),
                [(n, D), (k, KV), (n, KV), fit],
                square + [((D, KV), F32), ((KV, KV), F32), ((4 * n, KV), F32)],
                5, 3_000_000_000,
            )(after(pos, moves.token), *moves.stacks("K"))
            fit_kv = moves.passed(fit_kv)
        elif item == "kT":
            t_rows, s_rows = call(
                functools.partial(middle_kernel, n), [rows, rows], square, 6, 1_000_000_000
            )(after(pos, moves.token), x_rows, *moves.stacks("S"))
            t_rows = moves.passed(t_rows)
        else:
            new_gq, step_q, fit_q = call(
                functools.partial(right_kernel, n, width), [(n, D), (n, D), fit],
                square + [(rows, F32)], 7, 3_000_000_000,
            )(pos, t_rows, s_rows, *moves.stacks("G"))

    part = fit_q + fit_kv
    weight_q, weight_kv, moment_q, moment_kv = call(
        update_kernel, [(n, D), (n, KV)] * 2, [], 8, scalars=0, limit=8
    )(
        part, core_flip(part), step_q, step_kv,
        weight_query, weight_keyval, moment_query, moment_keyval,
    )
    return (new_aq, new_gq, new_akv, new_gkv, weight_q, weight_kv, moment_q, moment_kv)


def from_root(value, axis, source):
    kept = jnp.where(lax.axis_index(axis) == source, value, 0).astype(value.dtype)
    return lax.psum(kept, axis)


def newton(damped):
    extent = damped.shape[0]
    identity = jnp.eye(extent, dtype=jnp.float32)
    inverse_norm = 1.0 / jnp.max(jnp.sum(jnp.abs(damped), axis=1))
    iterate = inverse_norm * (2.0 * identity - inverse_norm * damped)
    product = jnp.dot(damped, iterate, precision=PRECISE)
    iterate = jnp.dot(iterate, 2.0 * identity - product, precision=PRECISE)
    return iterate


def damped_inverse(factor):
    extent = factor.shape[0]
    identity = jnp.eye(extent, dtype=jnp.float32)
    return newton(factor + DAMPING * jnp.trace(factor) / extent * identity)


def precondition(left_inverse, gradient, right_inverse):
    return jnp.dot(
        jnp.dot(left_inverse, gradient, precision=PRECISE), right_inverse, precision=PRECISE
    )


def inner_rows(first_block, second_block):
    return lax.dot_general(
        first_block, second_block, (((0,), (0,)), ((), ())), preferred_element_type=jnp.float32
    )


def deliver(matrix, holder):
    return from_root(matrix, ("dp", "group"), holder)


def owner_step(left_factor, right_factor, gradient):
    return precondition(damped_inverse(left_factor), gradient, damped_inverse(right_factor))


def shards(
    act_query,
    grad_query,
    act_keyval,
    grad_keyval,
    sample_rows,
    state_aq,
    state_gq,
    state_akv,
    state_gkv,
    weight_query,
    weight_keyval,
    moment_query,
    moment_keyval,
):
    devices = lax.axis_size("dp") * lax.axis_size("group")
    total_samples = sample_rows.shape[0] * devices
    flat_index = lax.axis_index("dp") * lax.axis_size("group") + lax.axis_index("group")
    extent = state_aq.shape[0]
    start = lax.axis_index("dp") * extent

    def covariance(tokens_block):
        chosen = jnp.take(tokens_block, sample_rows, axis=0)
        return inner_rows(chosen, chosen)

    local_terms = (
        covariance(act_query),
        covariance(grad_query),
        covariance(act_keyval),
        covariance(grad_keyval),
        inner_rows(act_query, grad_query),
        inner_rows(act_keyval, grad_keyval),
    )
    shares = (
        lax.psum_scatter(local_terms[0], "dp", scatter_dimension=0, tiled=True),
        lax.psum_scatter(local_terms[1], "dp", scatter_dimension=0, tiled=True),
        lax.psum_scatter(local_terms[2], "dp", scatter_dimension=0, tiled=True),
        lax.psum_scatter(local_terms[3], "dp", scatter_dimension=0, tiled=True),
        lax.psum_scatter(local_terms[4], "dp", scatter_dimension=0, tiled=True),
        lax.psum_scatter(local_terms[5], "dp", scatter_dimension=0, tiled=True),
    )
    totals = lax.psum((shares[0], shares[1], shares[2], shares[3], shares[4], shares[5]), "group")
    cov_aq, cov_gq, cov_akv, cov_gkv, rows_q, rows_kv = totals
    new_aq = BLEND_RATE * state_aq + (1.0 - BLEND_RATE) * (cov_aq / total_samples)
    new_gq = BLEND_RATE * state_gq + (1.0 - BLEND_RATE) * (cov_gq / total_samples)
    new_akv = BLEND_RATE * state_akv + (1.0 - BLEND_RATE) * (cov_akv / total_samples)
    new_gkv = BLEND_RATE * state_gkv + (1.0 - BLEND_RATE) * (cov_gkv / total_samples)
    gathered = (
        lax.all_gather(new_aq, "dp", axis=0, tiled=True),
        lax.all_gather(new_gq, "dp", axis=0, tiled=True),
        lax.all_gather(new_akv, "dp", axis=0, tiled=True),
        lax.all_gather(new_gkv, "dp", axis=0, tiled=True),
        lax.all_gather(rows_q, "dp", axis=0, tiled=True),
        lax.all_gather(rows_kv, "dp", axis=0, tiled=True),
    )
    whole_aq, whole_gq, whole_akv, whole_gkv, whole_sum_q, whole_sum_kv = gathered
    holders = (0, 0, 1, 1)
    pairs = (
        (whole_aq, whole_gq, whole_sum_q, rows_q, holders[0], holders[1]),
        (whole_akv, whole_gkv, whole_sum_kv, rows_kv, holders[2], holders[3]),
    )
    step_rows = []
    fitness = jnp.zeros((), jnp.float32)
    for left_factor, right_factor, gradient, gradient_rows, left_holder, right_holder in pairs:
        whole_step = lax.cond(
            flat_index == left_holder,
            owner_step,
            lambda first, second, third: jnp.zeros_like(third),
            left_factor,
            right_factor,
            gradient,
        )
        whole_step = deliver(whole_step, left_holder)
        fitness = fitness + jnp.sum(whole_step * gradient)
        step_rows.append(lax.dynamic_slice_in_dim(whole_step, start, extent, 0))
    scale = jnp.sqrt(TRUST_BOUND / (LEARNING_RATE * LEARNING_RATE * fitness))
    moment_q = MOMENTUM * moment_query + scale * step_rows[0]
    moment_kv = MOMENTUM * moment_keyval + scale * step_rows[1]
    weight_q = weight_query - LEARNING_RATE * moment_q
    weight_kv = weight_keyval - LEARNING_RATE * moment_kv
    return (new_aq, new_gq, new_akv, new_gkv, weight_q, weight_kv, moment_q, moment_kv)


def solution(mesh):
    placed = (
        P(("dp", "group"), None),
        P(("dp", "group"), None),
        P(("dp", "group"), None),
        P(("dp", "group"), None),
        P(("dp", "group")),
        P("dp", None),
        P("dp", None),
        P("dp", None),
        P("dp", None),
        P("dp", None),
        P("dp", None),
        P("dp", None),
        P("dp", None),
    )
    plane = mesh.shape["dp"] == 8 and mesh.shape["group"] == 4
    return jax.shard_map(
        fast_shards if plane else shards,
        mesh=mesh,
        in_specs=placed,
        out_specs=(
            P("dp", None),
            P("dp", None),
            P("dp", None),
            P("dp", None),
            P("dp", None),
            P("dp", None),
            P("dp", None),
            P("dp", None),
        ),
        check_vma=False,
    )
```

```python
import functools

import jax
import jax.numpy as jnp
from jax import lax
from jax.experimental import pallas as pl
from jax.experimental.pallas import tpu as pltpu
from jax.sharding import PartitionSpec as P

PRECISE = lax.Precision.HIGHEST
BLEND_RATE = 0.8
DAMPING = 0.05
MOMENTUM = 0.9
LEARNING_RATE = 0.001
TRUST_BOUND = 0.5
LANES = 128
F32 = jnp.float32
BF16 = jnp.bfloat16


def rolled(block, shift):
    return pltpu.roll(block, shift, 1)


def window_tiles(block, start, width):
    extent = block.shape[1]
    shift = lax.rem(extent - start, extent)
    turned = rolled(block, shift)
    return [turned[:, LANES * t:LANES * (t + 1)] for t in range(width // LANES)]


def plain_tiles(block):
    return [block[:, LANES * t:LANES * (t + 1)] for t in range(block.shape[1] // LANES)]


def write_tiles(ref, lead, tiles, at=0):
    for tile in tiles:
        ref[lead, at:at + tile.shape[0], :] = tile
        at += tile.shape[0]
    return at


def product(first, second):
    return lax.dot_general(
        first, second, (((1,), (0,)), ((), ())), preferred_element_type=F32
    )


def cast_kernel(rows, aq, gq, akv, gkv, out):
    at, tokens = 0, aq.shape[0]
    for ref in (aq, gq, akv, gkv):
        out[:tokens, at:at + ref.shape[1]] = ref[...].astype(F32)
        at += ref.shape[1]
    out[tokens:, :] = jnp.zeros((out.shape[0] - tokens, at), F32)
    out[tokens:tokens + 1, :rows.shape[1]] = rows[...].astype(F32)


def picker(all_tokens, tokens, samples):
    rows = all_tokens[tokens:tokens + 1, :samples].astype(jnp.int32)
    token = lax.broadcasted_iota(jnp.int32, (tokens, samples), 0)
    return (token == rows).astype(F32).T.astype(BF16)


def turned(values):
    return values.astype(F32).T.astype(BF16)


def own_kernel(
    tokens, samples, D,
    mine, y_aq, y_gq, y_akv, y_gkv, u_aq, u_gq, u_akv, u_gkv, t_q, t_kv, e_q, e_kv,
):
    pick = picker(mine, tokens, samples)
    at = 0
    for y, u in ((y_aq, u_aq), (y_gq, u_gq), (y_akv, u_akv), (y_gkv, u_gkv)):
        chosen = product(pick, mine[:tokens, at:at + y.shape[1]].astype(BF16))
        y[...] = chosen.astype(BF16)
        u[...] = chosen.T.astype(BF16)
        at += y.shape[1]
    t_q[...] = turned(mine[:tokens, :D])
    t_kv[...] = turned(mine[:tokens, 2 * D:3 * D])
    e_q[...] = mine[:tokens, D:2 * D].astype(BF16)
    e_kv[...] = mine[:tokens, 3 * D:].astype(BF16)


def roles(q, c):
    return [2 * chip + c for chip in (q, q ^ (1 + c), q ^ (2 - c), q ^ 3)]


def join(u, other, pick, own_u, own_y, lo, hi):
    samples, tokens = pick.shape
    chosen = product(pick, other[:tokens, lo:hi].astype(BF16))
    u[:, :samples] = own_u[...]
    u[:, samples:] = chosen.T.astype(BF16)
    return jnp.concatenate([own_y[...], chosen.astype(BF16)], axis=0)


def left_blocks(ref, n, blocks):
    parts = [ref[pl.ds(pl.multiple_of(n * b, 32), n), :] for b in blocks]
    return jnp.concatenate(parts, axis=0)


def four(values, n):
    return [values[n * r:n * (r + 1)] for r in range(4)]


def place(send, keep, tiles, at=0):
    write_tiles(send, 0, tiles[1], at)
    write_tiles(send, 1, tiles[3], at)
    write_tiles(keep, 0, tiles[0], at)
    return write_tiles(keep, 1, tiles[2], at)


def factor_tiles(u, y, state, n, blocks, width, scale):
    parts = four(product(left_blocks(u, n, blocks), y) * scale, n)
    parts[0] = parts[0] + (BLEND_RATE / 4.0) * state[...]
    return [window_tiles(part, n * b, width) for part, b in zip(parts, blocks)]


def gram_kernel(
    n, k, width, scale,
    pos, e_q, e_kv, other, y_aq, y_gq, y_akv, y_gkv, o_aq, o_gq, o_akv, o_gkv, o_q, o_kv,
    st_aq, st_gq, st_akv, st_gkv,
    a_send, a_keep, k_send, k_keep, s_send, s_keep, g_send, g_keep,
    u_aq, u_gq, u_akv, u_gkv, t_q, t_kv, g_kv,
):
    tokens, samples = o_kv.shape[1], o_akv.shape[1]
    D, KV = y_akv.shape[1], y_gkv.shape[1]
    blocks = roles(pos[0], pos[1])
    pick = picker(other, tokens, samples)

    def factor(u, o, y, state, lo):
        chosen = join(u, other, pick, o, y, lo, lo + D)
        return factor_tiles(u, chosen, state, n, blocks, width, scale)

    def gradient(t, o, lo, end, first, last):
        t[:, :tokens] = o[...]
        t[:, tokens:] = turned(other[:tokens, lo:lo + D])
        ends = [end[...], other[:tokens, first:last].astype(BF16)]
        return four(product(left_blocks(t, n, blocks), jnp.concatenate(ends, axis=0)), n)

    place(a_send, a_keep, factor(u_aq, o_aq, y_aq, st_aq, 0))
    at = place(k_send, k_keep, factor(u_akv, o_akv, y_akv, st_akv, 2 * D))
    sums = gradient(t_kv, o_kv, 2 * D, e_kv, 3 * D, 3 * D + KV)
    at = place(k_send, k_keep, [[part] for part in sums], at)
    chosen = join(u_gkv, other, pick, o_gkv, y_gkv, 3 * D, 3 * D + KV)
    g_kv[...] = product(u_gkv[...], chosen) * scale
    small = [g_kv[pl.ds(pl.multiple_of(k * b, 8), k), :] for b in blocks]
    small[0] = small[0] + (BLEND_RATE / 4.0) * st_gkv[...]
    place(k_send, k_keep, [[part] for part in small], at)
    place(s_send, s_keep, [plain_tiles(part) for part in gradient(t_q, o_q, 0, e_q, D, 2 * D)])
    place(g_send, g_keep, factor(u_gq, o_gq, y_gq, st_gq, D))


def identity_rows(rows, extent, start):
    row = lax.broadcasted_iota(jnp.int32, (rows, extent), 0) + start
    column = lax.broadcasted_iota(jnp.int32, (rows, extent), 1)
    return row == column


def scaled_inverse_terms(matrix):
    extent = matrix.shape[0]
    on_diagonal = identity_rows(extent, extent, 0)
    trace = jnp.sum(jnp.where(on_diagonal, matrix, 0.0))
    damped = matrix + jnp.where(on_diagonal, DAMPING * trace / extent, 0.0)
    c = 1.0 / jnp.max(jnp.sum(jnp.abs(damped), axis=1))
    return c, c * damped


def halves(values):
    high = values.astype(BF16)
    return high, (values - high.astype(F32)).astype(BF16)


def times(values, high, low):
    v_high, v_low = halves(values)
    rows = values.shape[0]
    stacked = product(jnp.concatenate([v_high, v_low], axis=0), high)
    return stacked[:rows] + stacked[rows:] + product(v_high, low)


def pieces_of(stacks, q, c):
    near, far = (roles(q, parity) for parity in (c, 1 - c))
    order = [(0, 0, 0), (0, 1, 2), (1, 0, 1), (1, 1, 3)]
    found = []
    for stack, blocks in ((stacks[:2], near), (stacks[2:], far)):
        found += [(stack[which].at[lead], blocks[role]) for which, lead, role in order]
    return found


def assemble(pieces, at, n, width, extent, whole):
    tiles = width // LANES
    for piece, b in pieces:
        parts = [piece[at + n * t:at + n * (t + 1), :] for t in range(tiles)]
        parts += [jnp.zeros((n, LANES), F32)] * (extent // LANES - tiles)
        turned = rolled(jnp.concatenate(parts, axis=1), n * b)
        whole[pl.ds(pl.multiple_of(n * b, 8), n), :] = turned
    windows = whole[...]

    def block_of(axis):
        shape = (extent, 1) if axis == 0 else (1, extent)
        index = lax.broadcasted_iota(jnp.int32, shape, axis)
        return sum([(index >= n * step).astype(jnp.int32) for step in range(1, 8)])

    apart = jnp.bitwise_and(block_of(1) - block_of(0), 7)
    matrix = jnp.where(apart <= 4, windows, windows.T)
    return matrix


def own_rows(ref, q, c, n):
    return ref[pl.ds(pl.multiple_of(n * (2 * q + c), 8), n), :]


def parity_rows(ref, c, n):
    parts = [ref[pl.ds(pl.multiple_of(n * (2 * j + c), 8), n), :] for j in range(4)]
    return jnp.concatenate(parts, axis=0)


def identity_parity(extent, c, n):
    parts = [identity_rows(n, extent, n * (2 * j + c)) for j in range(4)]
    return jnp.concatenate(parts, axis=0)


def left_rows(c, rows, identity, high, low):
    first = jnp.where(identity, 2.0, 0.0) - rows
    second = times(first, high, low)
    third = 2.0 * second - times(second, high, low)
    return c * (2.0 * first - third)


def right_product(values, c, high, low):
    first = 2.0 * values - times(values, high, low)
    second = times(first, high, low)
    third = 2.0 * second - times(second, high, low)
    return c * (2.0 * first - third)


def left_inverse(matrix, c, n, whole, high_ref, low_ref):
    factor, scaled = scaled_inverse_terms(matrix)
    whole[...] = scaled
    high_ref[...], low_ref[...] = halves(scaled)
    return left_rows(
        factor, parity_rows(whole, c, n), identity_parity(whole.shape[0], c, n),
        high_ref[...], low_ref[...],
    )


def left_kernel(n, width, pos, *refs):
    stacks, (new_ref, x_ref, whole, high_ref, low_ref) = refs[:4], refs[4:]
    q, c = pos[0], pos[1]
    matrix = assemble(pieces_of(stacks, q, c), 0, n, width, whole.shape[0], whole)
    whole[...] = matrix
    new_ref[...] = own_rows(whole, q, c, n)
    x_ref[...] = left_inverse(matrix, c, n, whole, high_ref, low_ref)


def middle_kernel(n, pos, x_ref, *refs):
    stacks, (t_ref, rows_ref, s_ref, s_high, s_low) = refs[:4], refs[4:]
    q, c = pos[0], pos[1]
    tiles = s_ref.shape[1] // LANES
    for piece, b in pieces_of(stacks, q, c):
        rows = jnp.concatenate([piece[n * t:n * (t + 1), :] for t in range(tiles)], axis=1)
        at = pl.ds(pl.multiple_of(n * b, 32), n)
        s_ref[at, :] = rows
        s_high[at, :], s_low[at, :] = halves(rows)
    t_ref[...] = times(x_ref[...], s_high[...], s_low[...])
    rows_ref[...] = parity_rows(s_ref, c, n)


def right_kernel(n, width, pos, t_ref, rows_ref, *refs):
    stacks, (new_ref, step_ref, fit_ref, whole, high_ref, low_ref, step_all) = refs[:4], refs[4:]
    q, c = pos[0], pos[1]
    matrix = assemble(pieces_of(stacks, q, c), 0, n, width, whole.shape[0], whole)
    whole[...] = matrix
    new_ref[...] = own_rows(whole, q, c, n)
    factor, scaled = scaled_inverse_terms(matrix)
    high_ref[...], low_ref[...] = halves(scaled)
    step = right_product(t_ref[...], factor, high_ref[...], low_ref[...])
    step_all[...] = step
    step_ref[...] = step_all[pl.ds(pl.multiple_of(n * q, 8), n), :]
    fit_ref[...] = jnp.broadcast_to(jnp.sum(step * rows_ref[...]), fit_ref.shape)


def keyval_kernel(n, k, width, pos, *refs):
    stacks, (new_left, new_right, step_ref, fit_ref) = refs[:4], refs[4:8]
    whole, high_ref, low_ref, grad_ref, g_ref, t_ref = refs[8:]
    q, c = pos[0], pos[1]
    pieces = pieces_of(stacks, q, c)
    at = n * (width // LANES)
    for piece, b in pieces:
        grad_ref[pl.ds(pl.multiple_of(n * b, 8), n), :] = piece[at:at + n, :]
        g_ref[pl.ds(pl.multiple_of(k * b, 8), k), :] = piece[at + n:at + n + k, :]
    matrix = assemble(pieces, 0, n, width, whole.shape[0], whole)
    whole[...] = matrix
    new_left[...] = own_rows(whole, q, c, n)
    new_right[...] = own_rows(g_ref, q, c, k)
    x_rows = left_inverse(matrix, c, n, whole, high_ref, low_ref)
    t_rows = times(x_rows, *halves(grad_ref[...]))
    factor, scaled = scaled_inverse_terms(g_ref[...])
    step = right_product(t_rows, factor, *halves(scaled))
    t_ref[...] = step
    step_ref[...] = t_ref[pl.ds(pl.multiple_of(n * q, 8), n), :]
    fit_ref[...] = jnp.broadcast_to(jnp.sum(step * parity_rows(grad_ref, c, n)), fit_ref.shape)


def update_kernel(fit_own, fit_other, *refs):
    (step_q, step_kv, weight_q, weight_kv, moment_q, moment_kv) = refs[:6]
    outs = refs[6:]
    fitness = (fit_own[...] + fit_other[...])[:1, :1]
    scale = jnp.sqrt(TRUST_BOUND / (LEARNING_RATE * LEARNING_RATE * fitness))
    for step, weight, moment, at in (
        (step_q, weight_q, moment_q, 0), (step_kv, weight_kv, moment_kv, 1)
    ):
        fresh = MOMENTUM * moment[...] + scale * step[...]
        outs[2 + at][...] = fresh
        outs[at][...] = weight[...] - LEARNING_RATE * fresh


def call(kernel, outs, scratch, count, flops=0, scalars=1, kind=F32, limit=24):
    vmem = pl.BlockSpec(memory_space=pltpu.VMEM)
    smem = pl.BlockSpec(memory_space=pltpu.SMEM)
    return pl.pallas_call(
        kernel,
        out_shape=[jax.ShapeDtypeStruct(shape, kind) for shape in outs],
        in_specs=[smem] * scalars + [vmem] * (count - scalars),
        out_specs=[vmem] * len(outs),
        scratch_shapes=[pltpu.VMEM(shape, kind) for shape, kind in scratch],
        compiler_params=pltpu.CompilerParams(vmem_limit_bytes=limit * 1024 * 1024),
        cost_estimate=pl.CostEstimate(flops=flops, bytes_accessed=4_000_000, transcendentals=0),
    )


def core_flip(value):
    return lax.ppermute(value, "dp", [(i, i ^ 1) for i in range(8)])


def first_hop(value):
    return lax.ppermute(value, "dp", [(i, i ^ (4 if i & 1 else 2)) for i in range(8)])


def second_hop(value):
    return lax.ppermute(value, "dp", [(i, i ^ (2 if i & 1 else 4)) for i in range(8)])


def plane_flip(value, bit):
    return lax.ppermute(value, "group", [(i, i ^ bit) for i in range(4)])


def after(value, *others):
    return lax.optimization_barrier((value,) + others)[0]


def plane_halves(piece):
    half = piece.shape[0] // 2
    even = lax.axis_index("group") % 2 == 0
    low, high = piece[:half], piece[half:]
    return jnp.where(even, low, high), jnp.where(even, high, low)


def plane_whole(mine, theirs):
    even = lax.axis_index("group") % 2 == 0
    return jnp.concatenate(
        [jnp.where(even, mine, theirs), jnp.where(even, theirs, mine)], axis=0
    )


ORDER = (
    "+Ars1", "+Krs1", "+Srs1", "-Ars1", "+Ars2", "-Krs1", "+Krs2", "-Ars2", "+Az1", "-Srs1",
    "+Srs2", "+Grs1", "-Krs2", "+Kz1", "-Az1", "+Az2", "-Srs2", "+Sz1", "-Kz1", "+Kz2", "-Grs1",
    "+Grs2", "-Az2", "+Az3", "-Sz1", "+Sz2", "-Grs2", "+Gz1", "-Az3", "+Aag1", "-Kz2", "+Kz3",
    "-Gz1", "+Gz2", "-Aag1", "+Acn", "+Aag2", "-Sz2", "+Sz3", "-Kz3", "-Acn", "+Kag1", "-Gz2",
    "+Gz3", "-Sz3", "+Sag1", "-Aag2", "+Acf", "-Kag1", "+Kcn", "+Kag2", "-Gz3", "-Acf", "+Gag1",
    "-Kcn", "kA", "-Sag1", "-Gag1", "+Scn", "+Sag2", "-Kag2", "+Kcf", "-Scn", "+Gcn", "+Gag2",
    "-Kcf", "kK", "-Gcn", "-Sag2", "+Scf", "-Gag2", "+Gcf", "-Scf", "kT", "-Gcf", "kG",
)


class Transfers:
    def __init__(self, sends, keeps):
        self.got = {}
        self.flying = {}
        self.sends, self.keeps = sends, keeps
        self.token = None

    def operand(self, chunk, step):
        got = self.got
        if step == "rs1":
            return self.sends[chunk]
        if step == "rs2":
            return self.keeps[chunk][1] + got[chunk, "rs1"][1]
        if step == "z1":
            own = self.keeps[chunk][0] + got[chunk, "rs1"][0] + got[chunk, "rs2"]
            got[chunk, "half"], theirs = plane_halves(own)
            return theirs
        if step == "z2":
            got[chunk, "half"] = got[chunk, "half"] + got[chunk, "z1"]
            return got[chunk, "half"]
        if step == "z3":
            got[chunk, "half"] = got[chunk, "half"] + got[chunk, "z2"]
            return got[chunk, "half"]
        if step == "ag1":
            got[chunk, "own"] = plane_whole(got[chunk, "half"], got[chunk, "z3"])
            return got[chunk, "own"]
        if step == "ag2":
            got[chunk, "near"] = jnp.stack([got[chunk, "own"], got[chunk, "ag1"]])
            return got[chunk, "near"]
        if step == "cn":
            if (chunk, "near") not in got:
                got[chunk, "near"] = jnp.stack([got[chunk, "own"], got[chunk, "ag1"]])
            return got[chunk, "near"]
        return got[chunk, "ag2"]

    hops = {
        "rs1": first_hop, "rs2": second_hop, "ag1": second_hop, "ag2": first_hop,
        "z1": lambda value: plane_flip(value, 1), "z2": lambda value: plane_flip(value, 2),
        "z3": lambda value: plane_flip(value, 1), "cn": core_flip, "cf": core_flip,
    }

    def start(self, chunk, step):
        value = self.operand(chunk, step)
        if self.token is not None:
            value = after(value, self.token)
        self.flying[chunk, step] = self.hops[step](value)

    def passed(self, value):
        if self.token is not None:
            value, _ = lax.optimization_barrier((value, self.token))
        self.token = value
        return value

    def wait(self, chunk, step):
        self.got[chunk, step] = self.passed(self.flying.pop((chunk, step)))

    def stacks(self, chunk):
        return [self.got[chunk, step] for step in ("near", "ag2", "cn", "cf")]


def fast_shards(
    act_query, grad_query, act_keyval, grad_keyval, sample_rows,
    state_aq, state_gq, state_akv, state_gkv,
    weight_query, weight_keyval, moment_query, moment_keyval,
):
    D, KV = act_query.shape[1], grad_keyval.shape[1]
    n, k = state_aq.shape[0], state_gkv.shape[0]
    tokens, samples = act_query.shape[0], sample_rows.shape[0]
    width = -(-5 * n // LANES) * LANES
    d = lax.axis_index("dp")
    pos = jnp.stack([d // 2, d % 2]).astype(jnp.int32)
    scale = (1.0 - BLEND_RATE) / (samples * 32)

    (mine,) = call(cast_kernel, [(tokens + 8, 3 * D + KV)], [], 5, scalars=0, limit=8)(
        sample_rows.reshape(1, samples), act_query, grad_query, act_keyval, grad_keyval
    )
    other = core_flip(mine)
    y_aq, y_gq, y_akv, y_gkv, u_aq, u_gq, u_akv, u_gkv, t_q, t_kv, e_q, e_kv = call(
        functools.partial(own_kernel, tokens, samples, D),
        [(samples, D)] * 3 + [(samples, KV)] + [(D, samples)] * 3 + [(KV, samples)]
        + [(D, tokens)] * 2 + [(tokens, D), (tokens, KV)],
        [], 1, 300_000_000, scalars=0, kind=BF16, limit=12,
    )(mine)

    r_f = n * (width // LANES)
    sizes = (r_f, r_f + n + k, n * (D // LANES), r_f)
    grams = call(
        functools.partial(gram_kernel, n, k, width, scale),
        [(2, size, LANES) for size in sizes for _ in range(2)],
        [
            *[((D, 2 * samples), BF16)] * 3, ((KV, 2 * samples), BF16),
            *[((D, 2 * tokens), BF16)] * 2, ((KV, KV), F32),
        ],
        18, 2_000_000_000, limit=16,
    )(
        pos, e_q, e_kv, other, y_aq, y_gq, y_akv, y_gkv, u_aq, u_gq, u_akv, u_gkv, t_q, t_kv,
        state_aq, state_gq, state_akv, state_gkv,
    )
    sends, keeps = dict(zip("AKSG", grams[0::2])), dict(zip("AKSG", grams[1::2]))

    rows = (4 * n, D)
    square = [((D, D), F32), ((D, D), BF16), ((D, D), BF16)]
    fit = (8, LANES)
    moves = Transfers(sends, keeps)
    for item in ORDER:
        if item[0] == "+":
            moves.start(item[1], item[2:])
        elif item[0] == "-":
            moves.wait(item[1], item[2:])
        elif item == "kA":
            new_aq, x_rows = call(
                functools.partial(left_kernel, n, width), [(n, D), rows], square, 5, 2_000_000_000
            )(after(pos, moves.token), *moves.stacks("A"))
            x_rows = moves.passed(x_rows)
        elif item == "kK":
            new_akv, new_gkv, step_kv, fit_kv = call(
                functools.partial(keyval_kernel, n, k, width),
                [(n, D), (k, KV), (n, KV), fit],
                square + [((D, KV), F32), ((KV, KV), F32), ((4 * n, KV), F32)],
                5, 3_000_000_000,
            )(after(pos, moves.token), *moves.stacks("K"))
            fit_kv = moves.passed(fit_kv)
        elif item == "kT":
            t_rows, s_rows = call(
                functools.partial(middle_kernel, n), [rows, rows], square, 6, 1_000_000_000
            )(after(pos, moves.token), x_rows, *moves.stacks("S"))
            t_rows = moves.passed(t_rows)
        else:
            new_gq, step_q, fit_q = call(
                functools.partial(right_kernel, n, width), [(n, D), (n, D), fit],
                square + [(rows, F32)], 7, 3_000_000_000,
            )(pos, t_rows, s_rows, *moves.stacks("G"))

    part = fit_q + fit_kv
    weight_q, weight_kv, moment_q, moment_kv = call(
        update_kernel, [(n, D), (n, KV)] * 2, [], 8, scalars=0, limit=8
    )(
        part, core_flip(part), step_q, step_kv,
        weight_query, weight_keyval, moment_query, moment_keyval,
    )
    return (new_aq, new_gq, new_akv, new_gkv, weight_q, weight_kv, moment_q, moment_kv)


def from_root(value, axis, source):
    kept = jnp.where(lax.axis_index(axis) == source, value, 0).astype(value.dtype)
    return lax.psum(kept, axis)


def newton(damped):
    extent = damped.shape[0]
    identity = jnp.eye(extent, dtype=jnp.float32)
    inverse_norm = 1.0 / jnp.max(jnp.sum(jnp.abs(damped), axis=1))
    iterate = inverse_norm * (2.0 * identity - inverse_norm * damped)
    product = jnp.dot(damped, iterate, precision=PRECISE)
    iterate = jnp.dot(iterate, 2.0 * identity - product, precision=PRECISE)
    return iterate


def damped_inverse(factor):
    extent = factor.shape[0]
    identity = jnp.eye(extent, dtype=jnp.float32)
    return newton(factor + DAMPING * jnp.trace(factor) / extent * identity)


def precondition(left_inverse, gradient, right_inverse):
    return jnp.dot(
        jnp.dot(left_inverse, gradient, precision=PRECISE), right_inverse, precision=PRECISE
    )


def inner_rows(first_block, second_block):
    return lax.dot_general(
        first_block, second_block, (((0,), (0,)), ((), ())), preferred_element_type=jnp.float32
    )


def deliver(matrix, holder):
    return from_root(matrix, ("dp", "group"), holder)


def owner_step(left_factor, right_factor, gradient):
    return precondition(damped_inverse(left_factor), gradient, damped_inverse(right_factor))


def shards(
    act_query,
    grad_query,
    act_keyval,
    grad_keyval,
    sample_rows,
    state_aq,
    state_gq,
    state_akv,
    state_gkv,
    weight_query,
    weight_keyval,
    moment_query,
    moment_keyval,
):
    devices = lax.axis_size("dp") * lax.axis_size("group")
    total_samples = sample_rows.shape[0] * devices
    flat_index = lax.axis_index("dp") * lax.axis_size("group") + lax.axis_index("group")
    extent = state_aq.shape[0]
    start = lax.axis_index("dp") * extent

    def covariance(tokens_block):
        chosen = jnp.take(tokens_block, sample_rows, axis=0)
        return inner_rows(chosen, chosen)

    local_terms = (
        covariance(act_query),
        covariance(grad_query),
        covariance(act_keyval),
        covariance(grad_keyval),
        inner_rows(act_query, grad_query),
        inner_rows(act_keyval, grad_keyval),
    )
    shares = (
        lax.psum_scatter(local_terms[0], "dp", scatter_dimension=0, tiled=True),
        lax.psum_scatter(local_terms[1], "dp", scatter_dimension=0, tiled=True),
        lax.psum_scatter(local_terms[2], "dp", scatter_dimension=0, tiled=True),
        lax.psum_scatter(local_terms[3], "dp", scatter_dimension=0, tiled=True),
        lax.psum_scatter(local_terms[4], "dp", scatter_dimension=0, tiled=True),
        lax.psum_scatter(local_terms[5], "dp", scatter_dimension=0, tiled=True),
    )
    totals = lax.psum((shares[0], shares[1], shares[2], shares[3], shares[4], shares[5]), "group")
    cov_aq, cov_gq, cov_akv, cov_gkv, rows_q, rows_kv = totals
    new_aq = BLEND_RATE * state_aq + (1.0 - BLEND_RATE) * (cov_aq / total_samples)
    new_gq = BLEND_RATE * state_gq + (1.0 - BLEND_RATE) * (cov_gq / total_samples)
    new_akv = BLEND_RATE * state_akv + (1.0 - BLEND_RATE) * (cov_akv / total_samples)
    new_gkv = BLEND_RATE * state_gkv + (1.0 - BLEND_RATE) * (cov_gkv / total_samples)
    gathered = (
        lax.all_gather(new_aq, "dp", axis=0, tiled=True),
        lax.all_gather(new_gq, "dp", axis=0, tiled=True),
        lax.all_gather(new_akv, "dp", axis=0, tiled=True),
        lax.all_gather(new_gkv, "dp", axis=0, tiled=True),
        lax.all_gather(rows_q, "dp", axis=0, tiled=True),
        lax.all_gather(rows_kv, "dp", axis=0, tiled=True),
    )
    whole_aq, whole_gq, whole_akv, whole_gkv, whole_sum_q, whole_sum_kv = gathered
    holders = (0, 0, 1, 1)
    pairs = (
        (whole_aq, whole_gq, whole_sum_q, rows_q, holders[0], holders[1]),
        (whole_akv, whole_gkv, whole_sum_kv, rows_kv, holders[2], holders[3]),
    )
    step_rows = []
    fitness = jnp.zeros((), jnp.float32)
    for left_factor, right_factor, gradient, gradient_rows, left_holder, right_holder in pairs:
        whole_step = lax.cond(
            flat_index == left_holder,
            owner_step,
            lambda first, second, third: jnp.zeros_like(third),
            left_factor,
            right_factor,
            gradient,
        )
        whole_step = deliver(whole_step, left_holder)
        fitness = fitness + jnp.sum(whole_step * gradient)
        step_rows.append(lax.dynamic_slice_in_dim(whole_step, start, extent, 0))
    scale = jnp.sqrt(TRUST_BOUND / (LEARNING_RATE * LEARNING_RATE * fitness))
    moment_q = MOMENTUM * moment_query + scale * step_rows[0]
    moment_kv = MOMENTUM * moment_keyval + scale * step_rows[1]
    weight_q = weight_query - LEARNING_RATE * moment_q
    weight_kv = weight_keyval - LEARNING_RATE * moment_kv
    return (new_aq, new_gq, new_akv, new_gkv, weight_q, weight_kv, moment_q, moment_kv)


def solution(mesh):
    placed = (
        P(("dp", "group"), None),
        P(("dp", "group"), None),
        P(("dp", "group"), None),
        P(("dp", "group"), None),
        P(("dp", "group")),
        P("dp", None),
        P("dp", None),
        P("dp", None),
        P("dp", None),
        P("dp", None),
        P("dp", None),
        P("dp", None),
        P("dp", None),
    )
    plane = mesh.shape["dp"] == 8 and mesh.shape["group"] == 4
    return jax.shard_map(
        fast_shards if plane else shards,
        mesh=mesh,
        in_specs=placed,
        out_specs=(
            P("dp", None),
            P("dp", None),
            P("dp", None),
            P("dp", None),
            P("dp", None),
            P("dp", None),
            P("dp", None),
            P("dp", None),
        ),
        check_vma=False,
    )
```
